128 devices in a mesh: gx: 4 (over x_lo, core), gy: 8 (over z, x_hi), gz: 4 (over y).
Axes of the slice: x: 4 (x_hi: 2, x_lo: 2; x = x_hi * 2 + x_lo), y: 4, z: 4, core: 2. Of those that a mesh axis runs over, the one named last changes fastest.
Arguments:
- inputs: bfloat16 [3072, 6144], P('gy', ('gz', 'gx')), may hold values from -6 to 6
- weight: bfloat16 [6144, 24576], P('gz', ('gx', 'gy')), may hold values from -0.078125 to 0.078125
- cotangent: bfloat16 [3072, 24576], P('gy', ('gx', 'gz')), may hold values from -3 to 3
Outputs:
- activation: bfloat16 [3072, 24576], P('gy', ('gx', 'gz'))
- input_grad: bfloat16 [3072, 6144], P('gy', ('gz', 'gx'))
- weight_grad: bfloat16 [6144, 24576], P('gz', ('gx', 'gy'))
The draws below stay inside these ranges and needn't reach their ends.
All inputs are finite; a program needn't handle non-finite values.
Results may differ from the reference program's by a relative error of at most 0.02.
Values may be sent and summed in bfloat16 or wider, within the bound.
A program may use at most 192 MiB of HBM per device.

```python
import jax
import jax.numpy as jnp
from jax import lax

D = 6144
FF = 24576
TOKENS = 3072
N_GX = 4
N_GY = 8
N_GZ = 4


def block_scale(stream_key, shape, cuts, smallest, high):
    gain, own = 1.0, jax.random.fold_in(stream_key, 6)
    for position, blocks in cuts:
        steps = jnp.exp(jax.random.uniform(jax.random.fold_in(own, position), (blocks,), jnp.float32, smallest / len(cuts), high / len(cuts)))
        gain = gain * jnp.repeat(steps, shape[position] // blocks).reshape([-1 if axis == position else 1 for axis in range(len(shape))])
    return gain


def centred(rng, extent, deviation, most, pieces=(), dtype=jnp.bfloat16):
    values = deviation * jax.random.normal(rng, extent, jnp.float32)
    if pieces:
        values = values * block_scale(rng, extent, pieces, -0.22, 0.18)
    return jnp.clip(values, -most, most).astype(dtype)


def setup_inputs(seed: int = 0) -> dict:
    key_list = jax.random.split(jax.random.key(seed), 4)
    inputs = centred(key_list[0], (TOKENS, D), 1.0, 6.0, ((0, 8), (1, 16)))
    weight = centred(key_list[1], (D, FF), D ** -0.5, 0.078125, ((0, 4), (1, 32)))
    cotangent = centred(key_list[2], (TOKENS, FF), 0.2, 3.0, ((0, 8), (1, 16)))
    return dict(inputs=inputs, weight=weight, cotangent=cotangent)


def gelu_tanh(value):
    return jax.nn.gelu(value, approximate=True)

def rounded(value):
    return lax.optimization_barrier(value.astype(jnp.bfloat16)).astype(jnp.float32)

def reference(inputs, weight, cotangent):
    width = D // N_GZ
    preact = jnp.zeros((TOKENS, FF), jnp.float32)
    for group in range(N_GZ):
        part = jnp.dot(inputs[:, group * width:(group + 1) * width], weight[group * width:(group + 1) * width, :], preferred_element_type=jnp.float32)
        preact = preact + rounded(part)
    output, slope_fn = jax.vjp(gelu_tanh, preact)
    activation = output.astype(jnp.bfloat16)
    slopes = slope_fn(cotangent.astype(jnp.float32))[0].astype(jnp.bfloat16)
    hidden = FF // N_GX
    input_sum = jnp.zeros((TOKENS, D), jnp.float32)
    for group in range(N_GX):
        part = lax.dot_general(slopes[:, group * hidden:(group + 1) * hidden], weight[:, group * hidden:(group + 1) * hidden], (((1,), (1,)), ((), ())), preferred_element_type=jnp.float32)
        input_sum = input_sum + rounded(part)
    tokens_per = TOKENS // N_GY
    weight_sum = jnp.zeros((D, FF), jnp.float32)
    for group in range(N_GY):
        part = lax.dot_general(inputs[group * tokens_per:(group + 1) * tokens_per, :], slopes[group * tokens_per:(group + 1) * tokens_per, :], (((0,), (0,)), ((), ())), preferred_element_type=jnp.float32)
        weight_sum = weight_sum + rounded(part)
    return (activation, input_sum.astype(jnp.bfloat16), weight_sum.astype(jnp.bfloat16))
```

```python
import functools

import jax
import jax.numpy as jnp
from jax import lax
from jax.experimental import pallas as pl
from jax.experimental.pallas import tpu as pltpu
from jax.sharding import PartitionSpec as P

MESH = pl.DeviceIdType.MESH
F32, BF16 = jnp.float32, jnp.bfloat16
RING = 4
SPANS = (16, 32, 32, 16)
OWN = sum(SPANS)
STARTS = tuple(sum(SPANS[:k]) for k in range(len(SPANS)))
CHUNKS = range(len(SPANS))
HID = 768
FEAT = 384
N_SEM = 320
N_LOCAL = 40


def part_of(first, step):
    return pl.ds(first, step)


class Device:
    def __init__(self):
        gx, gy, gz = (lax.axis_index(name) for name in ("gx", "gy", "gz"))
        self.core = gx % 2
        self.at = {"x": (gy % 2) * 2 + gx // 2, "y": gz, "z": gy // 2}

    def name(self, core=None, **at):
        at = {**self.at, **at}
        core = self.core if core is None else core
        return {"gx": (at["x"] % 2) * 2 + core, "gy": at["z"] * 2 + at["x"] // 2, "gz": at["y"]}

    def along(self, axis, step):
        return (self.at[axis] + step) % RING


def cols(x):
    return pl.ds(pl.multiple_of((x % 2) * FEAT, FEAT), FEAT)


def gelu_and_slope(value, cotangent):
    scale, cubic = 0.7978845608028654, 0.044715
    square = value * value
    t = jnp.tanh(scale * value * (1.0 + cubic * square))
    half = 0.5 * (1.0 + t)
    slope = half + 0.5 * value * ((1.0 + t) * (1.0 - t)) * (scale + (3.0 * cubic * scale) * square)
    return value * half, cotangent * slope


def add_into(dst, *srcs):
    total = dst[...].astype(F32)
    for src in srcs:
        total = total + src[...].astype(F32)
    dst[...] = total.astype(BF16)


def add_rows(dst, *srcs):
    def step(i, carry):
        add_into(dst.at[i], *(src.at[i] for src in srcs))
        return carry

    lax.fori_loop(0, dst.shape[0], step, 0)


class Moves:
    def __init__(self, device, send, recv, local):
        self.device, self.send, self.recv, self.local = device, send, recv, local
        self.count = self.locals = 0
        self.sent = []

    def start(self, src, dst, **to):
        j = self.count
        self.count += 1
        copy = pltpu.make_async_remote_copy(
            src_ref=src, dst_ref=dst, send_sem=self.send.at[j], recv_sem=self.recv.at[j],
            device_id=self.device.name(**to), device_id_type=MESH,
        )
        copy.start()
        self.sent.append(copy)
        return copy

    def here(self, src, dst):
        j = self.locals
        self.locals += 1
        copy = pltpu.make_async_copy(src, dst, self.local.at[j])
        copy.start()
        return copy

    def drain(self):
        for copy in self.sent:
            copy.wait_send()
        self.sent = []


class Gather:
    def __init__(self, moves, axis, slot, own=None):
        self.m, self.axis, self.slot = moves, axis, slot
        self.own = own or (lambda part: slot(moves.device.at[axis], part))

    def begin(self):
        d, a = self.m.device, self.axis
        me = d.at[a]
        up, down = {a: d.along(a, 1)}, {a: d.along(a, 3)}
        self.up0 = self.m.start(self.own(0), self.slot(me, 0), **up)
        self.down1 = self.m.start(self.own(1), self.slot(me, 1), **down)
        self.up1 = self.m.start(self.own(1), self.slot(me, 1), **up)
        self.down0 = self.m.start(self.own(0), self.slot(me, 0), **down)

    def forward(self):
        d, a = self.m.device, self.axis
        self.up0.wait_recv()
        view = self.slot(d.along(a, 3), 0)
        self.far0 = self.m.start(view, view, **{a: d.along(a, 1)})
        self.down1.wait_recv()
        view = self.slot(d.along(a, 1), 1)
        self.far1 = self.m.start(view, view, **{a: d.along(a, 3)})

    def end(self):
        for copy in (self.up1, self.down0, self.far0, self.far1):
            copy.wait_recv()


class Reduce:
    def __init__(self, moves, axis, piece, far, near, add):
        self.m, self.axis, self.piece, self.far, self.near, self.add = moves, axis, piece, far, near, add

    def begin(self):
        d, a, p = self.m.device, self.axis, self.piece
        up, down, across = d.along(a, 1), d.along(a, 3), d.along(a, 2)
        self.far0 = self.m.start(p(across, 0), self.far.at[0], **{a: up})
        self.far1 = self.m.start(p(across, 1), self.far.at[1], **{a: down})
        self.up1 = self.m.start(p(up, 1), self.near.at[0, 1], **{a: up})
        self.down0 = self.m.start(p(down, 0), self.near.at[1, 0], **{a: down})

    def middle(self):
        d, a, p = self.m.device, self.axis, self.piece
        up, down = d.along(a, 1), d.along(a, 3)
        self.far0.wait_recv()
        self.add(p(up, 0), self.far.at[0])
        self.up0 = self.m.start(p(up, 0), self.near.at[0, 0], **{a: up})
        self.far1.wait_recv()
        self.add(p(down, 1), self.far.at[1])
        self.down1 = self.m.start(p(down, 1), self.near.at[1, 1], **{a: down})

    def arrive(self):
        for copy in (self.up0, self.up1, self.down0, self.down1):
            copy.wait_recv()

    def end(self):
        self.arrive()
        me = self.m.device.at[self.axis]
        for part in range(2):
            self.add(self.piece(me, part), self.near.at[0, part], self.near.at[1, part])


def scratch_of():
    shapes = {}
    for k in CHUNKS:
        r = SPANS[k]
        block = (4, 2, 4, r, HID)
        for name, shape in dict(
            x=(2, *block), p=block, s=block, d=(2, *block), core=block,
            yfar=(2, 2, 2, r, HID), ynear=(2, 2, 2, 2, r, HID),
            axfar=(2, 2, 2, r, FEAT), axnear=(2, 2, 2, 2, r, FEAT),
            azfar=(2, 1, r, FEAT), aznear=(2, 2, 1, r, FEAT),
            bzfar=(2, 1, 2, r, HID), bznear=(2, 2, 1, 2, r, HID),
            bxfar=(2, 1, r, FEAT), bxnear=(2, 2, 1, r, FEAT),
        ).items():
            shapes.setdefault(name, []).append(shape)
    return shapes


NAMES = tuple(scratch_of())


def kernel(in_ref, w_ref, cot_ref, act_ref, dx_ref, dw_ref, *scratch):
    bufs, rest = {}, list(scratch)
    for name in NAMES:
        bufs[name] = [rest.pop(0) for _ in CHUNKS]
    w, acc, dw, cot1, cot, act, act1, send, recv, local = rest
    dev = Device()
    core, at = dev.core, dev.at
    x, y, z = at["x"], at["y"], at["z"]
    half = x // 2
    m = Moves(dev, send, recv, local)
    plane = [(dz, dh) for dz in range(4) for dh in range(2) if (dz, dh) != (0, 0)]

    def in_plane(dz, dh):
        return dict(z=(z + dz) % RING, x=((half + dh) % 2) * 2 + x % 2)

    w_copies = [m.here(w_ref.at[lo, c], w.at[c, pl.ds(lo * FEAT, FEAT)]) for c in range(2) for lo in range(2)]
    own_copies = [
        m.here(in_ref.at[:, pl.ds(STARTS[k], SPANS[k])], bufs["x"][k].at[core, z, half, :, :, cols(x)]) for k in CHUNKS
    ]

    barrier = pltpu.get_barrier_semaphore()
    peers = [dict(core=1 - core), dict(x=dev.along("x", 1)), dict(x=dev.along("x", 3))]
    peers += [dict(y=dev.along("y", s)) for s in (1, 2, 3)] + [in_plane(*step) for step in plane]
    for peer in peers:
        pl.semaphore_signal(barrier, inc=1, device_id=dev.name(**peer), device_id_type=MESH)
    pl.semaphore_wait(barrier, len(peers))

    gathers = {}

    def input_gathers(k):
        b = bufs["x"][k]
        rows = pl.ds(STARTS[k], SPANS[k])

        def own(first):
            return lambda part: in_ref.at[pl.ds(first + part, 1), rows]

        gathers[k] = dict(
            ax=Gather(m, "x", lambda q, part: b.at[core, z, q // 2, pl.ds(part, 1), :, cols(q)], own(0)),
            az=Gather(m, "z", lambda q, part: b.at[core, q, part, pl.ds(0, 2)]),
            bz=Gather(m, "z", lambda q, part: b.at[core, q, half, pl.ds(2 + part, 1), :, cols(x)], own(2)),
            bx=Gather(m, "x", lambda q, part: b.at[core, pl.ds(2 * part, 2), q // 2, pl.ds(2, 2), :, cols(q)]),
        )

    def xa(k, stage):
        b = bufs["x"][k]
        if stage == 0:
            input_gathers(k)
            g = gathers[k]
            g["ax"].begin()
            g["bz"].begin()
        g = gathers[k]
        if stage == 1:
            g["ax"].forward()
            g["bz"].forward()
        if stage == 2:
            own_copies[k].wait()
            g["ax"].end()
            g["az"].begin()
            g["bz"].end()
            g["bx"].begin()
        if stage == 3:
            g["az"].forward()
            g["bx"].forward()
        if stage == 4:
            g["az"].end()
            view = b.at[core, :, :, pl.ds(0, 2)]
            g["core0"] = m.start(view, view, core=1 - core)
            g["bx"].end()
            view = b.at[core, :, :, pl.ds(2, 2)]
            g["core1"] = m.start(view, view, core=1 - core)
        if stage == 5:
            g["core0"].wait_recv()
            g["core1"].wait_recv()

    cot_moves = {}

    def cot_y():
        cot_moves["own"] = m.here(cot_ref.at[y], cot1.at[y])
        cot_moves["y"] = [
            m.start(cot_ref.at[dev.along("y", s)], cot1.at[y], y=dev.along("y", s)) for s in (1, 2, 3)
        ]

    def cot_plane():
        cot_moves["own"].wait()
        for copy in cot_moves["y"]:
            copy.wait_recv()

        def source(to):
            return cot1.at[to["z"], :, pl.ds(pl.multiple_of((to["x"] // 2) * HID, HID), HID)]

        cot_moves["plane"] = [m.start(source(in_plane(*step)), cot.at[z, half], **in_plane(*step)) for step in plane]
        cot_moves["plane_own"] = m.here(source(dict(z=z, x=x)), cot.at[z, half])

    def cot_end():
        cot_moves["plane_own"].wait()
        for copy in cot_moves["plane"]:
            copy.wait_recv()

    act_moves = {}

    def act_plane(first, count):
        rows = pl.ds(first, count)
        dst = act1.at[z, rows, pl.ds(pl.multiple_of(half * HID, HID), HID)]
        act_moves[first] = [
            m.start(act.at[to["z"], to["x"] // 2, rows], dst, **to) for to in (in_plane(*step) for step in plane)
        ], m.here(act.at[z, half, rows], dst)

    def act_y(first, count):
        rows = pl.ds(first, count)
        remote, mine = act_moves[first]
        mine.wait()
        for copy in remote:
            copy.wait_recv()
        act_moves[first] = [
            m.start(act1.at[dev.along("y", s), rows], act_ref.at[y, rows], y=dev.along("y", s)) for s in (1, 2, 3)
        ], m.here(act1.at[y, rows], act_ref.at[y, rows])

    def act_end(first):
        remote, mine = act_moves[first]
        mine.wait()
        for copy in remote:
            copy.wait_recv()

    sums = {}

    def project(k):
        b, p, r = bufs["x"][k], bufs["p"][k], SPANS[k]
        if k == 0:
            for copy in w_copies:
                copy.wait()

        def tile(n, carry):
            where = pl.ds(pl.multiple_of(n * 256, 256), 256)
            total = jnp.dot(b[0].reshape(32 * r, HID), w[0, :, where], preferred_element_type=F32)
            total += jnp.dot(b[1].reshape(32 * r, HID), w[1, :, where], preferred_element_type=F32)
            p[:, :, :, :, where] = total.astype(BF16).reshape(4, 2, 4, r, 256)
            return carry

        lax.fori_loop(0, 3, tile, 0)
        sums[k] = Reduce(
            m, "y", lambda q, part: p.at[pl.ds(2 * part, 2), :, q], bufs["yfar"][k], bufs["ynear"][k], add_rows
        )
        sums[k].begin()

    spread = {}

    def gelu(k):
        p, s, near, r = bufs["p"][k], bufs["s"][k], bufs["ynear"][k], SPANS[k]
        sums[k].arrive()
        rows = pl.ds(STARTS[k], r)

        def step(i, carry):
            zz, hh = i // 2, i % 2
            value = p[zz, hh, y].astype(F32)
            value = value + near[0, zz // 2, zz % 2, hh].astype(F32) + near[1, zz // 2, zz % 2, hh].astype(F32)
            a, slope = gelu_and_slope(value, cot[zz, hh, rows].astype(F32))
            act[zz, hh, rows] = a.astype(BF16)
            s[zz, hh, y] = slope.astype(BF16)
            return carry

        lax.fori_loop(0, 8, step, 0)
        spread[k] = Gather(m, "y", lambda q, part: s.at[pl.ds(2 * part, 2), :, q])
        spread[k].begin()

    crossing = {}

    def input_terms(k):
        s, d, r = bufs["s"][k], bufs["d"][k], SPANS[k]
        spread[k].end()

        def one(c):
            def tile(n, carry):
                where = pl.ds(pl.multiple_of(n * 256, 256), 256)
                total = lax.dot_general(
                    s[...].reshape(32 * r, HID), w[c, where, :], (((1,), (1,)), ((), ())), preferred_element_type=F32
                )
                d[c, :, :, :, :, where] = total.astype(BF16).reshape(4, 2, 4, r, 256)
                return carry

            lax.fori_loop(0, 3, tile, 0)

        one(1 - core)
        crossing[k] = m.start(d.at[1 - core], bufs["core"][k], core=1 - core)
        one(core)

    def weight_terms(k):
        b, s, r = bufs["x"][k], bufs["s"][k], SPANS[k]

        def tile(n, carry):
            c = n // 3
            where = pl.ds(pl.multiple_of((n % 3) * 256, 256), 256)
            total = lax.dot_general(
                b[c, :, :, :, :, where].reshape(32 * r, 256), s[...].reshape(32 * r, HID),
                (((0,), (0,)), ((), ())), preferred_element_type=F32,
            )
            if k > 0:
                total = total + acc[c, where, :]
            if k < len(SPANS) - 1:
                acc[c, where, :] = total
            else:
                dw[c, where, :] = total.astype(BF16)
            return carry

        lax.fori_loop(0, 6, tile, 0)

    def weight_out():
        return [m.here(dw.at[c, pl.ds(lo * FEAT, FEAT)], dw_ref.at[lo, c]) for c in range(2) for lo in range(2)]

    backs = {}

    def dxs(k, stage):
        d, r = bufs["d"][k], SPANS[k]
        if stage == 0:
            crossing[k].wait_recv()
            add_rows(d.at[core], bufs["core"][k])
            backs[k] = dict(
                ax=Reduce(m, "x", lambda q, part: d.at[core, pl.ds(2 * part, 2), q // 2, pl.ds(0, 2), :, cols(q)],
                          bufs["axfar"][k], bufs["axnear"][k], add_into),
                bz=Reduce(m, "z", lambda q, part: d.at[core, q, pl.ds(part, 1), pl.ds(2, 2)],
                          bufs["bzfar"][k], bufs["bznear"][k], add_into),
                az=Reduce(m, "z", lambda q, part: d.at[core, q, half, pl.ds(part, 1), :, cols(x)],
                          bufs["azfar"][k], bufs["aznear"][k], add_into),
                bx=Reduce(m, "x", lambda q, part: d.at[core, z, q // 2, pl.ds(2 + part, 1), :, cols(q)],
                          bufs["bxfar"][k], bufs["bxnear"][k], add_into),
            )
            backs[k]["ax"].begin()
            backs[k]["bz"].begin()
        g = backs[k]
        if stage == 1:
            g["ax"].middle()
            g["bz"].middle()
        if stage == 2:
            g["ax"].end()
            g["az"].begin()
            g["bz"].end()
            g["bx"].begin()
        if stage == 3:
            g["az"].middle()
            g["bx"].middle()
        if stage == 4:
            g["az"].end()
            g["bx"].end()
            dx_ref[:, pl.ds(STARTS[k], r), :] = d[core, z, half, :, :, cols(x)]

    last = len(SPANS) - 1
    xa(0, 0)
    cot_y()
    xa(0, 1)
    xa(0, 2)
    xa(1, 0)
    xa(0, 3)
    xa(1, 1)
    xa(0, 4)
    xa(1, 2)
    xa(0, 5)
    project(0)
    xa(1, 3)
    cot_plane()
    xa(1, 4)
    sums[0].middle()
    xa(2, 0)
    xa(1, 5)
    project(1)
    xa(2, 1)
    cot_end()
    for k in CHUNKS:
        gelu(k)
        if k + 1 <= last:
            sums[k + 1].middle()
        if k + 2 <= last:
            xa(k + 2, 2)
            xa(k + 2, 3)
            if k + 3 <= last:
                xa(k + 3, 0)
        spread[k].forward()
        if k + 2 <= last:
            xa(k + 2, 4)
            xa(k + 2, 5)
            project(k + 2)
            if k + 3 <= last:
                xa(k + 3, 1)
        if k == last - 1:
            act_plane(0, STARTS[last])
        if k >= 1:
            dxs(k - 1, 1)
            dxs(k - 1, 2)
        if k == last:
            act_plane(STARTS[last], SPANS[last])
        input_terms(k)
        dxs(k, 0)
        if k >= 1:
            dxs(k - 1, 3)
        weight_terms(k)
        if k >= 1:
            dxs(k - 1, 4)
    act_y(0, STARTS[last])
    act_y(STARTS[last], SPANS[last])
    outs = weight_out()
    for stage in (1, 2, 3, 4):
        dxs(last, stage)
    act_end(0)
    act_end(STARTS[last])
    for copy in outs:
        copy.wait()
    m.drain()


def on_device(inputs, weight, cotangent):
    shapes = [pltpu.VMEM(shape, BF16) for name, each in scratch_of().items() for shape in each]
    act, dx, dw = pl.pallas_call(
        kernel,
        out_shape=(
            jax.ShapeDtypeStruct((4, OWN, 2 * HID), BF16),
            jax.ShapeDtypeStruct((4, OWN, FEAT), BF16),
            jax.ShapeDtypeStruct((2, 2, FEAT, HID), BF16),
        ),
        in_specs=[
            pl.BlockSpec(memory_space=pltpu.VMEM),
            pl.BlockSpec(memory_space=pl.ANY),
            pl.BlockSpec(memory_space=pl.ANY),
        ],
        out_specs=(
            pl.BlockSpec(memory_space=pl.ANY),
            pl.BlockSpec(memory_space=pltpu.VMEM),
            pl.BlockSpec(memory_space=pl.ANY),
        ),
        scratch_shapes=[
            *shapes,
            pltpu.VMEM((2, HID, HID), BF16),
            pltpu.VMEM((2, HID, HID), F32),
            pltpu.VMEM((2, HID, HID), BF16),
            pltpu.VMEM((4, OWN, 2 * HID), BF16),
            pltpu.VMEM((4, 2, OWN, HID), BF16),
            pltpu.VMEM((4, 2, OWN, HID), BF16),
            pltpu.VMEM((4, OWN, 2 * HID), BF16),
            pltpu.SemaphoreType.DMA((N_SEM,)),
            pltpu.SemaphoreType.DMA((N_SEM,)),
            pltpu.SemaphoreType.DMA((N_LOCAL,)),
        ],
        compiler_params=pltpu.CompilerParams(
            collective_id=0, has_side_effects=True, vmem_limit_bytes=62 * 2**20
        ),
        cost_estimate=pl.CostEstimate(flops=6 * 384 * 1536 * 6144, bytes_accessed=8 * 2**20, transcendentals=0),
    )(
        inputs.reshape(4, OWN, FEAT),
        weight.reshape(2, 2, FEAT, HID),
        cotangent.reshape(4, OWN, 2 * HID),
    )
    return act.reshape(4 * OWN, 2 * HID), dx.reshape(4 * OWN, FEAT), dw.reshape(4 * FEAT, HID)


def solution(mesh):
    return jax.shard_map(
        on_device,
        mesh=mesh,
        in_specs=(P("gy", ("gz", "gx")), P("gz", ("gx", "gy")), P("gy", ("gx", "gz"))),
        out_specs=(P("gy", ("gx", "gz")), P("gy", ("gz", "gx")), P("gz", ("gx", "gy"))),
        check_vma=False,
    )
```

```python
import functools

import jax
import jax.numpy as jnp
from jax import lax
from jax.experimental import pallas as pl
from jax.experimental.pallas import tpu as pltpu
from jax.sharding import PartitionSpec as P

MESH = pl.DeviceIdType.MESH
F32, BF16 = jnp.float32, jnp.bfloat16
RING = 4
SPANS = (16, 16, 16, 16, 16, 16)
OWN = sum(SPANS)
STARTS = tuple(sum(SPANS[:k]) for k in range(len(SPANS)))
CHUNKS = range(len(SPANS))
HID = 768
FEAT = 384
N_SEM = 512
N_LOCAL = 64
COT_PARTS = ((0, 1), (1, 6))
ACT_PARTS = ((0, 5), (5, 6))
DIRECT_IN = (0, 1, 2, 3, 4, 5)
DIRECT_OUT = (0, 1, 2, 3, 4, 5)
ORDER = (
    ("ax0", 0), ("bz0", 0), ("bz0", 1), ("bz0", 2), ("ax0", 1), ("ax0", 2), ("c0", 0), ("c0", 1), ("ax0", 3),
    ("bz0", 3), ("ax2", 0), ("bz2", 0), ("ax2", 1), ("bz2", 1), ("bz0", 4), ("bz2", 2), ("ax2", 2),
    ("bz0", 5), ("c1", 0), ("az2", 0), ("bx2", 0), ("ax0", 4), ("P", 0), ("az2", 1), ("bz2", 3), ("ax2", 3),
    ("bx2", 1), ("P", 1), ("c1", 1), ("R1a", 0), ("bx2", 2), ("az2", 2), ("R1b", 0), ("P", 2), ("G", 0),
    ("ax0", 5), ("bz2", 5), ("R1b", 2), ("bx2", 3), ("R1a", 1), ("R1a", 2), ("az2", 3), ("ax2", 4),
    ("A1a", 0), ("R1b", 1), ("bz2", 4), ("P", 3), ("A1b", 0), ("G", 2), ("ax2", 5), ("G", 1), ("Dh", 0),
    ("Dl", 0), ("A1a", 2), ("az2", 4), ("az2", 5), ("bx2", 4), ("R1a", 3), ("bx2", 5), ("A1b", 2), ("dx0", 0),
    ("P", 4), ("P", 5), ("Dh", 2), ("Dl", 2), ("rz2", 0), ("dx0", 2), ("R1b", 3), ("rx2", 0), ("R1a", 4),
    ("R1b", 4), ("R1b", 5), ("A1a", 1), ("W", 0), ("A1b", 1), ("R1a", 5), ("G", 4), ("rz2", 2), ("G", 3),
    ("p0", 0), ("Dh", 1), ("Dl", 1), ("rx2", 2), ("A1b", 4), ("A1a", 4), ("dx0", 1), ("W", 1), ("A1a", 3),
    ("A1b", 3), ("G", 5), ("W", 2), ("p0", 1), ("sz2", 0), ("Dh", 4), ("Dl", 4), ("Dh", 3), ("dx0", 4),
    ("A1b", 5), ("A1a", 5), ("p1", 0), ("W", 3), ("Dl", 3), ("dx0", 3), ("Dh", 5), ("sz2", 2), ("Dl", 5),
    ("rz2", 4), ("p1", 1), ("dx0", 5), ("rx2", 4), ("W", 4), ("sx2", 0), ("rz2", 1), ("rx2", 3), ("rz2", 3),
    ("W", 5), ("rx2", 1), ("sx2", 2), ("rz2", 5), ("rx2", 5), ("sz2", 4), ("sx2", 4), ("sz2", 1), ("sx2", 3),
    ("sx2", 1), ("p2", 0), ("sz2", 3), ("p2", 1), ("sx2", 5), ("sz2", 5),
)


class Device:
    def __init__(self):
        gx, gy, gz = (lax.axis_index(name) for name in ("gx", "gy", "gz"))
        self.core = gx % 2
        self.at = {"x": (gy % 2) * 2 + gx // 2, "y": gz, "z": gy // 2}

    def name(self, core=None, **at):
        at = {**self.at, **at}
        core = self.core if core is None else core
        return {"gx": (at["x"] % 2) * 2 + core, "gy": at["z"] * 2 + at["x"] // 2, "gz": at["y"]}

    def along(self, axis, step):
        return (self.at[axis] + step) % RING


def cols(x):
    return pl.ds(pl.multiple_of((x % 2) * FEAT, FEAT), FEAT)


def gelu_and_slope(value, cotangent):
    scale, cubic = 0.7978845608028654, 0.044715
    square = value * value
    t = jnp.tanh(scale * value * (1.0 + cubic * square))
    half = 0.5 * (1.0 + t)
    slope = half + 0.5 * value * ((1.0 + t) * (1.0 - t)) * (scale + (3.0 * cubic * scale) * square)
    return value * half, cotangent * slope


def add_into(dst, *srcs):
    total = dst[...].astype(F32)
    for src in srcs:
        total = total + src[...].astype(F32)
    dst[...] = total.astype(BF16)


def add_rows(dst, *srcs):
    def step(i, carry):
        add_into(dst.at[i], *(src.at[i] for src in srcs))
        return carry

    lax.fori_loop(0, dst.shape[0], step, 0)


class Moves:
    def __init__(self, device, send, recv, local):
        self.device, self.send, self.recv, self.local = device, send, recv, local
        self.count = self.locals = 0
        self.sent = []

    def start(self, src, dst, **to):
        j = self.count
        self.count += 1
        copy = pltpu.make_async_remote_copy(
            src_ref=src, dst_ref=dst, send_sem=self.send.at[j], recv_sem=self.recv.at[j],
            device_id=self.device.name(**to), device_id_type=MESH,
        )
        copy.start()
        self.sent.append(copy)
        return copy

    def here(self, src, dst):
        j = self.locals
        self.locals += 1
        copy = pltpu.make_async_copy(src, dst, self.local.at[j])
        copy.start()
        return copy

    def drain(self):
        for copy in self.sent:
            copy.wait_send()
        self.sent = []


class Gather:
    def __init__(self, moves, axis, slot, own=None, direct=False):
        self.m, self.axis, self.slot, self.direct = moves, axis, slot, direct
        self.own = own or (lambda part: slot(moves.device.at[axis], part))

    def begin(self):
        d, a = self.m.device, self.axis
        me = d.at[a]
        if self.direct:
            self.copies = [
                self.m.start(self.own(part), self.slot(me, part), **{a: d.along(a, step)})
                for part in range(2) for step in (1, 3, 2)
            ]
            return
        up, down = {a: d.along(a, 1)}, {a: d.along(a, 3)}
        self.up0 = self.m.start(self.own(0), self.slot(me, 0), **up)
        self.down1 = self.m.start(self.own(1), self.slot(me, 1), **down)
        self.up1 = self.m.start(self.own(1), self.slot(me, 1), **up)
        self.down0 = self.m.start(self.own(0), self.slot(me, 0), **down)

    def forward_up(self):
        d, a = self.m.device, self.axis
        self.up0.wait_recv()
        view = self.slot(d.along(a, 3), 0)
        self.far0 = self.m.start(view, view, **{a: d.along(a, 1)})

    def forward_down(self):
        d, a = self.m.device, self.axis
        self.down1.wait_recv()
        view = self.slot(d.along(a, 1), 1)
        self.far1 = self.m.start(view, view, **{a: d.along(a, 3)})

    def end(self):
        for copy in self.copies if self.direct else (self.up1, self.down0, self.far0, self.far1):
            copy.wait_recv()


class Reduce:
    def __init__(self, moves, axis, piece, far, near, add, direct=False):
        self.m, self.axis, self.piece, self.far, self.near, self.add = moves, axis, piece, far, near, add
        self.direct = direct

    def begin(self):
        d, a, p = self.m.device, self.axis, self.piece
        up, down, across = d.along(a, 1), d.along(a, 3), d.along(a, 2)
        if self.direct:
            self.copies = [
                self.m.start(p(to, part), land, **{a: to})
                for part in range(2)
                for to, land in ((up, self.near.at[0, part]), (down, self.near.at[1, part]), (across, self.far.at[part]))
            ]
            return
        self.far0 = self.m.start(p(across, 0), self.far.at[0], **{a: up})
        self.far1 = self.m.start(p(across, 1), self.far.at[1], **{a: down})
        self.up1 = self.m.start(p(up, 1), self.near.at[0, 1], **{a: up})
        self.down0 = self.m.start(p(down, 0), self.near.at[1, 0], **{a: down})

    def middle_up(self):
        d, a, p = self.m.device, self.axis, self.piece
        up = d.along(a, 1)
        self.far0.wait_recv()
        self.add(p(up, 0), self.far.at[0])
        self.up0 = self.m.start(p(up, 0), self.near.at[0, 0], **{a: up})

    def middle_down(self):
        d, a, p = self.m.device, self.axis, self.piece
        down = d.along(a, 3)
        self.far1.wait_recv()
        self.add(p(down, 1), self.far.at[1])
        self.down1 = self.m.start(p(down, 1), self.near.at[1, 1], **{a: down})

    def arrive(self):
        for copy in self.copies if self.direct else (self.up0, self.up1, self.down0, self.down1):
            copy.wait_recv()

    def end(self):
        self.arrive()
        me = self.m.device.at[self.axis]
        for part in range(2):
            more = (self.far.at[part],) if self.direct else ()
            self.add(self.piece(me, part), self.near.at[0, part], self.near.at[1, part], *more)


def scratch_of():
    shapes = {}
    for k in CHUNKS:
        r = SPANS[k]
        block = (4, 2, 4, r, HID)
        for name, shape in dict(
            x=(2, *block), p=block, s=block, d=(2, *block), core=block,
            yfar=(2, 2, 2, r, HID), ynear=(2, 2, 2, 2, r, HID),
            axfar=(2, 2, 2, r, FEAT), axnear=(2, 2, 2, 2, r, FEAT),
            azfar=(2, 1, r, FEAT), aznear=(2, 2, 1, r, FEAT),
            bzfar=(2, 1, 2, r, HID), bznear=(2, 2, 1, 2, r, HID),
            bxfar=(2, 1, r, FEAT), bxnear=(2, 2, 1, r, FEAT),
        ).items():
            shapes.setdefault(name, []).append(shape)
    return shapes


NAMES = tuple(scratch_of())


def kernel(in_ref, w_ref, cot_ref, act_ref, dx_ref, dw_ref, *scratch):
    bufs, rest = {}, list(scratch)
    for name in NAMES:
        bufs[name] = [rest.pop(0) for _ in CHUNKS]
    w, acc, dw, cot1, cot, act, act1, send, recv, local = rest
    dev = Device()
    core, at = dev.core, dev.at
    x, y, z = at["x"], at["y"], at["z"]
    half = x // 2
    m = Moves(dev, send, recv, local)
    plane = [(dz, dh) for dz in range(4) for dh in range(2) if (dz, dh) != (0, 0)]

    def in_plane(dz, dh):
        return dict(z=(z + dz) % RING, x=((half + dh) % 2) * 2 + x % 2)

    w_copies = [m.here(w_ref.at[lo, c], w.at[c, pl.ds(lo * FEAT, FEAT)]) for c in range(2) for lo in range(2)]
    own_copies = [
        m.here(in_ref.at[:, pl.ds(STARTS[k], SPANS[k])], bufs["x"][k].at[core, z, half, :, :, cols(x)]) for k in CHUNKS
    ]

    barrier = pltpu.get_barrier_semaphore()
    peers = [dict(core=1 - core), dict(x=dev.along("x", 1)), dict(x=dev.along("x", 3))]
    peers += [dict(y=dev.along("y", s)) for s in (1, 2, 3)] + [in_plane(*step) for step in plane]
    for peer in peers:
        pl.semaphore_signal(barrier, inc=1, device_id=dev.name(**peer), device_id_type=MESH)
    pl.semaphore_wait(barrier, len(peers))

    tasks = {}

    def task(name):
        def keep(step):
            tasks[name] = step
            return step

        return keep

    def input_tasks(k):
        b = bufs["x"][k]
        rows = pl.ds(STARTS[k], SPANS[k])

        def own(first):
            return lambda part: in_ref.at[pl.ds(first + part, 1), rows]

        ax = Gather(m, "x", lambda q, part: b.at[core, z, q // 2, pl.ds(part, 1), :, cols(q)], own(0), k in DIRECT_IN)
        az = Gather(m, "z", lambda q, part: b.at[core, q, part, pl.ds(0, 2)], direct=k in DIRECT_IN)
        bz = Gather(m, "z", lambda q, part: b.at[core, q, half, pl.ds(2 + part, 1), :, cols(x)], own(2), k in DIRECT_IN)
        bx = Gather(m, "x", lambda q, part: b.at[core, pl.ds(2 * part, 2), q // 2, pl.ds(2, 2), :, cols(q)],
                    direct=k in DIRECT_IN)
        passed = {}

        def turn(name, first, second):
            @task((name, k))
            def _():
                if k not in landed:
                    own_copies[k].wait()
                    landed.add(k)
                first.end()
                second.begin()

        def give(name, last, first_row):
            @task((name, k))
            def _():
                last.end()
                view = b.at[core, :, :, pl.ds(first_row, 2)]
                passed[name] = m.start(view, view, core=1 - core)

        for name, ring in (("ax1", ax), ("bz1", bz), ("az1", az), ("bx1", bx)):
            tasks[name + "a", k] = ring.forward_up
            tasks[name + "b", k] = ring.forward_down
        tasks["ax0", k], tasks["bz0", k] = ax.begin, bz.begin
        turn("ax2", ax, az)
        turn("bz2", bz, bx)
        give("az2", az, 0)
        give("bx2", bx, 2)
        return passed

    landed = set()
    passed = [input_tasks(k) for k in CHUNKS]

    def rows_of(part):
        first, end = part
        return pl.ds(STARTS[first], sum(SPANS[first:end]))

    cot_moves = {}

    def cot_tasks(i):
        rows = rows_of(COT_PARTS[i])

        @task(("c0", i))
        def _():
            cot_moves[i] = [m.here(cot_ref.at[y, rows], cot1.at[y, rows])], [
                m.start(cot_ref.at[dev.along("y", s), rows], cot1.at[y, rows], y=dev.along("y", s)) for s in (1, 2, 3)
            ]

        @task(("c1", i))
        def _():
            wait_all(cot_moves[i])

            def source(to):
                return cot1.at[to["z"], rows, pl.ds(pl.multiple_of((to["x"] // 2) * HID, HID), HID)]

            dst = cot.at[z, half, rows]
            cot_moves[i] = [m.here(source(at), dst)], [
                m.start(source(to), dst, **to) for to in (in_plane(*step) for step in plane)
            ]

    def wait_all(moves):
        here, remote = moves
        for copy in here:
            copy.wait()
        for copy in remote:
            copy.wait_recv()

    for i in range(len(COT_PARTS)):
        cot_tasks(i)

    act_moves = {}

    def act_tasks(i):
        rows = rows_of(ACT_PARTS[i])

        @task(("p0", i))
        def _():
            dst = act1.at[z, rows, pl.ds(pl.multiple_of(half * HID, HID), HID)]
            act_moves[i] = [m.here(act.at[z, half, rows], dst)], [
                m.start(act.at[to["z"], to["x"] // 2, rows], dst, **to) for to in (in_plane(*step) for step in plane)
            ]

        @task(("p1", i))
        def _():
            wait_all(act_moves[i])
            act_moves[i] = [m.here(act1.at[y, rows], act_ref.at[y, rows])], [
                m.start(act1.at[dev.along("y", s), rows], act_ref.at[y, rows], y=dev.along("y", s)) for s in (1, 2, 3)
            ]

        @task(("p2", i))
        def _():
            wait_all(act_moves[i])

    for i in range(len(ACT_PARTS)):
        act_tasks(i)

    def main_tasks(k):
        b, p, s, d, near = (bufs[name][k] for name in ("x", "p", "s", "d", "ynear"))
        r, rows = SPANS[k], pl.ds(STARTS[k], SPANS[k])
        total = Reduce(m, "y", lambda q, part: p.at[pl.ds(2 * part, 2), :, q], bufs["yfar"][k], near, add_rows)
        spread = Gather(m, "y", lambda q, part: s.at[pl.ds(2 * part, 2), :, q])
        state = {}

        @task(("P", k))
        def _():
            for copy in passed[k].values():
                copy.wait_recv()
            while w_copies:
                w_copies.pop().wait()

            def tile(n, carry):
                where = pl.ds(pl.multiple_of(n * 256, 256), 256)
                value = jnp.dot(b[0].reshape(32 * r, HID), w[0, :, where], preferred_element_type=F32)
                value += jnp.dot(b[1].reshape(32 * r, HID), w[1, :, where], preferred_element_type=F32)
                p[:, :, :, :, where] = value.astype(BF16).reshape(4, 2, 4, r, 256)
                return carry

            lax.fori_loop(0, 3, tile, 0)
            total.begin()

        tasks["R1a", k], tasks["R1b", k] = total.middle_up, total.middle_down

        @task(("G", k))
        def _():
            total.arrive()
            for i, (first, end) in enumerate(COT_PARTS):
                if first <= k < end and i in cot_moves:
                    wait_all(cot_moves.pop(i))

            def step(i, carry):
                zz, hh = i // 2, i % 2
                value = p[zz, hh, y].astype(F32)
                value = value + near[0, zz // 2, zz % 2, hh].astype(F32) + near[1, zz // 2, zz % 2, hh].astype(F32)
                a, slope = gelu_and_slope(value, cot[zz, hh, rows].astype(F32))
                act[zz, hh, rows] = a.astype(BF16)
                s[zz, hh, y] = slope.astype(BF16)
                return carry

            lax.fori_loop(0, 8, step, 0)
            spread.begin()

        tasks["A1a", k], tasks["A1b", k] = spread.forward_up, spread.forward_down

        def input_terms(c):
            def tile(n, carry):
                where = pl.ds(pl.multiple_of(n * 256, 256), 256)
                value = lax.dot_general(
                    s[...].reshape(32 * r, HID), w[c, where, :], (((1,), (1,)), ((), ())), preferred_element_type=F32
                )
                d[c, :, :, :, :, where] = value.astype(BF16).reshape(4, 2, 4, r, 256)
                return carry

            lax.fori_loop(0, 3, tile, 0)

        @task(("Dh", k))
        def _():
            spread.end()
            input_terms(1 - core)
            state["cross"] = m.start(d.at[1 - core], bufs["core"][k], core=1 - core)

        @task(("Dl", k))
        def _():
            input_terms(core)

        @task(("W", k))
        def _():
            def tile(n, carry):
                c = n // 3
                where = pl.ds(pl.multiple_of((n % 3) * 256, 256), 256)
                value = lax.dot_general(
                    b[c, :, :, :, :, where].reshape(32 * r, 256), s[...].reshape(32 * r, HID),
                    (((0,), (0,)), ((), ())), preferred_element_type=F32,
                )
                if k > 0:
                    value = value + acc[c, where, :]
                if k < last:
                    acc[c, where, :] = value
                else:
                    dw[c, where, :] = value.astype(BF16)
                return carry

            lax.fori_loop(0, 6, tile, 0)
            if k == last:
                for c in range(2):
                    for lo in range(2):
                        outs.append(m.here(dw.at[c, pl.ds(lo * FEAT, FEAT)], dw_ref.at[lo, c]))

        ax = Reduce(m, "x", lambda q, part: d.at[core, pl.ds(2 * part, 2), q // 2, pl.ds(0, 2), :, cols(q)],
                    bufs["axfar"][k], bufs["axnear"][k], add_into, k in DIRECT_OUT)
        bz = Reduce(m, "z", lambda q, part: d.at[core, q, pl.ds(part, 1), pl.ds(2, 2)],
                    bufs["bzfar"][k], bufs["bznear"][k], add_into, k in DIRECT_OUT)
        az = Reduce(m, "z", lambda q, part: d.at[core, q, half, pl.ds(part, 1), :, cols(x)],
                    bufs["azfar"][k], bufs["aznear"][k], add_into, k in DIRECT_OUT)
        bx = Reduce(m, "x", lambda q, part: d.at[core, z, q // 2, pl.ds(2 + part, 1), :, cols(q)],
                    bufs["bxfar"][k], bufs["bxnear"][k], add_into, k in DIRECT_OUT)
        for name, ring in (("rx1", ax), ("rz1", bz), ("sz1", az), ("sx1", bx)):
            tasks[name + "a", k] = ring.middle_up
            tasks[name + "b", k] = ring.middle_down

        @task(("dx0", k))
        def _():
            state["cross"].wait_recv()
            add_rows(d.at[core], bufs["core"][k])
            ax.begin()
            bz.begin()

        @task(("rx2", k))
        def _():
            ax.end()
            az.begin()

        @task(("rz2", k))
        def _():
            bz.end()
            bx.begin()

        @task(("sz2", k))
        def _():
            az.end()
            dx_ref[0:2, rows, :] = d[core, z, half, 0:2, :, cols(x)]

        @task(("sx2", k))
        def _():
            bx.end()
            dx_ref[2:4, rows, :] = d[core, z, half, 2:4, :, cols(x)]

    last, outs = len(SPANS) - 1, []
    for k in CHUNKS:
        main_tasks(k)
    for step in ORDER:
        tasks[step]()
    for copy in outs:
        copy.wait()
    m.drain()


def on_device(inputs, weight, cotangent):
    shapes = [pltpu.VMEM(shape, BF16) for name, each in scratch_of().items() for shape in each]
    act, dx, dw = pl.pallas_call(
        kernel,
        out_shape=(
            jax.ShapeDtypeStruct((4, OWN, 2 * HID), BF16),
            jax.ShapeDtypeStruct((4, OWN, FEAT), BF16),
            jax.ShapeDtypeStruct((2, 2, FEAT, HID), BF16),
        ),
        in_specs=[
            pl.BlockSpec(memory_space=pltpu.VMEM),
            pl.BlockSpec(memory_space=pl.ANY),
            pl.BlockSpec(memory_space=pl.ANY),
        ],
        out_specs=(
            pl.BlockSpec(memory_space=pl.ANY),
            pl.BlockSpec(memory_space=pltpu.VMEM),
            pl.BlockSpec(memory_space=pl.ANY),
        ),
        scratch_shapes=[
            *shapes,
            pltpu.VMEM((2, HID, HID), BF16),
            pltpu.VMEM((2, HID, HID), F32),
            pltpu.VMEM((2, HID, HID), BF16),
            pltpu.VMEM((4, OWN, 2 * HID), BF16),
            pltpu.VMEM((4, 2, OWN, HID), BF16),
            pltpu.VMEM((4, 2, OWN, HID), BF16),
            pltpu.VMEM((4, OWN, 2 * HID), BF16),
            pltpu.SemaphoreType.DMA((N_SEM,)),
            pltpu.SemaphoreType.DMA((N_SEM,)),
            pltpu.SemaphoreType.DMA((N_LOCAL,)),
        ],
        compiler_params=pltpu.CompilerParams(
            collective_id=0, has_side_effects=True, vmem_limit_bytes=62 * 2**20
        ),
        cost_estimate=pl.CostEstimate(flops=6 * 384 * 1536 * 6144, bytes_accessed=8 * 2**20, transcendentals=0),
    )(
        inputs.reshape(4, OWN, FEAT),
        weight.reshape(2, 2, FEAT, HID),
        cotangent.reshape(4, OWN, 2 * HID),
    )
    return act.reshape(4 * OWN, 2 * HID), dx.reshape(4 * OWN, FEAT), dw.reshape(4 * FEAT, HID)


def solution(mesh):
    return jax.shard_map(
        on_device,
        mesh=mesh,
        in_specs=(P("gy", ("gz", "gx")), P("gz", ("gx", "gy")), P("gy", ("gx", "gz"))),
        out_specs=(P("gy", ("gx", "gz")), P("gy", ("gz", "gx")), P("gz", ("gx", "gy"))),
        check_vma=False,
    )
```

```python
import functools

import jax
import jax.numpy as jnp
from jax import lax
from jax.experimental import pallas as pl
from jax.experimental.pallas import tpu as pltpu
from jax.sharding import PartitionSpec as P

MESH = pl.DeviceIdType.MESH
F32, BF16 = jnp.float32, jnp.bfloat16
RING = 4
SPANS = (16, 16, 16, 16, 16, 16)
OWN = sum(SPANS)
STARTS = tuple(sum(SPANS[:k]) for k in range(len(SPANS)))
CHUNKS = range(len(SPANS))
HID = 768
FEAT = 384
COT_PARTS = ((0, 1), (1, 6))
ACT_PARTS = ((0, 5), (5, 6))
N_SEM = 17 * len(SPANS) + 2 * (len(COT_PARTS) + len(ACT_PARTS)) + 2
ORDER = (
    ("bz0", 0), ("c0", 0), ("ax0", 0), ("ax0", 2), ("bz0", 2), ("ax0", 1), ("bz0", 3), ("bz0", 1), ("bz2", 0),
    ("c0", 1), ("ax2", 0), ("ax2", 1), ("bz0", 4), ("bz2", 1), ("ax0", 4), ("ax2", 2), ("ax0", 3), ("bx2", 0),
    ("bz2", 2), ("az2", 0), ("c1", 0), ("P", 0), ("bx2", 1), ("az2", 1), ("P", 1), ("az2", 2), ("bz2", 3),
    ("bz2", 4), ("bz0", 5), ("bx2", 2), ("R1a", 0), ("ax2", 4), ("ax2", 3), ("ax0", 5), ("R1b", 0), ("P", 2),
    ("R1a", 1), ("G", 0), ("bx2", 3), ("c1", 1), ("R1a", 2), ("az2", 4), ("R1b", 1), ("az2", 3), ("bx2", 4),
    ("R1b", 2), ("P", 3), ("P", 4), ("ax2", 5), ("A1b", 0), ("A1a", 0), ("R1a", 3), ("bz2", 5), ("G", 2),
    ("R1b", 4), ("R1a", 4), ("G", 1), ("R1b", 3), ("Dh", 0), ("bx2", 5), ("A1b", 2), ("az2", 5), ("Dl", 0),
    ("dx0", 0), ("P", 5), ("A1a", 2), ("W", 0), ("A1b", 1), ("A1a", 1), ("G", 4), ("G", 3), ("p0", 0),
    ("rx2", 0), ("Dh", 2), ("Dh", 1), ("W", 1), ("R1a", 5), ("R1b", 5), ("Dl", 2), ("dx0", 2), ("rz2", 0),
    ("A1b", 3), ("A1a", 3), ("Dl", 1), ("sz2", 0), ("A1a", 4), ("dx0", 1), ("A1b", 4), ("W", 2), ("G", 5),
    ("p0", 1), ("Dh", 3), ("W", 3), ("Dl", 3), ("dx0", 3), ("A1b", 5), ("A1a", 5), ("p1", 0), ("Dh", 4),
    ("Dl", 4), ("rx2", 1), ("rz2", 1), ("dx0", 4), ("Dh", 5), ("sx2", 0), ("Dl", 5), ("dx0", 5), ("rz2", 3),
    ("p1", 1), ("rx2", 2), ("rx2", 3), ("W", 4), ("rz2", 2), ("rz2", 4), ("W", 5), ("rx2", 4), ("rz2", 5),
    ("rx2", 5), ("sz2", 1), ("p2", 0), ("sz2", 3), ("p2", 1), ("sx2", 1), ("sx2", 3), ("sx2", 4), ("sx2", 2),
    ("sz2", 2), ("sz2", 4), ("sx2", 5), ("sz2", 5),
)


class Device:
    def __init__(self):
        gx, gy, gz = (lax.axis_index(name) for name in ("gx", "gy", "gz"))
        self.core = gx % 2
        self.at = {"x": (gy % 2) * 2 + gx // 2, "y": gz, "z": gy // 2}

    def name(self, core=None, **at):
        at = {**self.at, **at}
        core = self.core if core is None else core
        return {"gx": (at["x"] % 2) * 2 + core, "gy": at["z"] * 2 + at["x"] // 2, "gz": at["y"]}

    def along(self, axis, step):
        return (self.at[axis] + step) % RING


def cols(x):
    return pl.ds(pl.multiple_of((x % 2) * FEAT, FEAT), FEAT)


def gelu_and_slope(value, cotangent):
    scale, cubic = 0.7978845608028654, 0.044715
    square = value * value
    t = jnp.tanh(scale * value * (1.0 + cubic * square))
    half = 0.5 * (1.0 + t)
    slope = half + 0.5 * value * ((1.0 + t) * (1.0 - t)) * (scale + (3.0 * cubic * scale) * square)
    return value * half, cotangent * slope


def add_into(dst, *srcs):
    total = dst[...].astype(F32)
    for src in srcs:
        total = total + src[...].astype(F32)
    dst[...] = total.astype(BF16)


def add_rows(dst, *srcs):
    def step(i, carry):
        add_into(dst.at[i], *(src.at[i] for src in srcs))
        return carry

    lax.fori_loop(0, dst.shape[0], step, 0)


class Moves:
    def __init__(self, device, send, recv):
        self.device, self.send, self.recv = device, send, recv
        self.count = 0
        self.sent = []

    def sem(self):
        self.count += 1
        return self.recv.at[self.count - 1]

    def start(self, src, dst, sem, **to):
        copy = pltpu.make_async_remote_copy(
            src_ref=src, dst_ref=dst, send_sem=self.send, recv_sem=sem,
            device_id=self.device.name(**to), device_id_type=MESH,
        )
        copy.start()
        self.sent.append(copy)

    def here(self, src, dst, sem):
        pltpu.make_async_copy(src, dst, sem).start()

    def wait(self, size, sem):
        pltpu.make_async_copy(size, size, sem).wait()

    def drain(self):
        for copy in self.sent:
            copy.wait_send()
        self.sent = []


class Straight:
    def __init__(self, moves, axis, size):
        self.m, self.axis, self.size, self.sem = moves, axis, size, moves.sem()

    def send(self, src, dst):
        for step in (1, 3, 2):
            to = self.m.device.along(self.axis, step)
            self.m.start(src(to), dst(step), self.sem, **{self.axis: to})

    def arrive(self):
        self.m.wait(self.size, self.sem)


class Gather:
    def __init__(self, moves, axis, slot, rest):
        self.m, self.axis, self.slot, self.rest = moves, axis, slot, rest
        self.up_sem, self.down_sem, self.rest_sem = moves.sem(), moves.sem(), moves.sem()

    def begin(self):
        d, a = self.m.device, self.axis
        me, up, down = d.at[a], {a: d.along(a, 1)}, {a: d.along(a, 3)}
        first, second = self.slot(me, 0), self.slot(me, 1)
        self.m.start(first, first, self.up_sem, **up)
        self.m.start(second, second, self.down_sem, **down)
        self.m.start(second, second, self.rest_sem, **up)
        self.m.start(first, first, self.rest_sem, **down)

    def forward_up(self):
        d, a = self.m.device, self.axis
        view = self.slot(d.along(a, 3), 0)
        self.m.wait(view, self.up_sem)
        self.m.start(view, view, self.rest_sem, **{a: d.along(a, 1)})

    def forward_down(self):
        d, a = self.m.device, self.axis
        view = self.slot(d.along(a, 1), 1)
        self.m.wait(view, self.down_sem)
        self.m.start(view, view, self.rest_sem, **{a: d.along(a, 3)})

    def end(self):
        self.m.wait(self.rest, self.rest_sem)


class Reduce:
    def __init__(self, moves, axis, piece, far, near):
        self.m, self.axis, self.piece, self.far, self.near = moves, axis, piece, far, near
        self.up_sem, self.down_sem, self.near_sem = moves.sem(), moves.sem(), moves.sem()

    def begin(self):
        d, a, p = self.m.device, self.axis, self.piece
        up, down, across = d.along(a, 1), d.along(a, 3), d.along(a, 2)
        self.m.start(p(across, 0), self.far.at[0], self.up_sem, **{a: up})
        self.m.start(p(across, 1), self.far.at[1], self.down_sem, **{a: down})
        self.m.start(p(up, 1), self.near.at[0, 1], self.near_sem, **{a: up})
        self.m.start(p(down, 0), self.near.at[1, 0], self.near_sem, **{a: down})

    def middle_up(self):
        d, a = self.m.device, self.axis
        up = d.along(a, 1)
        self.m.wait(self.far.at[0], self.up_sem)
        add_rows(self.piece(up, 0), self.far.at[0])
        self.m.start(self.piece(up, 0), self.near.at[0, 0], self.near_sem, **{a: up})

    def middle_down(self):
        d, a = self.m.device, self.axis
        down = d.along(a, 3)
        self.m.wait(self.far.at[1], self.down_sem)
        add_rows(self.piece(down, 1), self.far.at[1])
        self.m.start(self.piece(down, 1), self.near.at[1, 1], self.near_sem, **{a: down})

    def arrive(self):
        self.m.wait(self.near, self.near_sem)


def scratch_of():
    shapes = {}
    for k in CHUNKS:
        r = SPANS[k]
        block = (4, 2, 4, r, HID)
        for name, shape in dict(
            x=(2, *block), p=block, s=block, d=(2, *block), core=block,
            yfar=(2, 2, 2, r, HID), ynear=(2, 2, 2, 2, r, HID),
            ax=(3, 4, 2, r, FEAT), az=(3, 2, r, FEAT), bz=(3, 2, 2, r, HID), bx=(3, 2, r, FEAT),
        ).items():
            shapes.setdefault(name, []).append(shape)
    return shapes


NAMES = tuple(scratch_of())


def kernel(in_ref, w_ref, cot_ref, act_ref, dx_ref, dw_ref, *scratch):
    bufs, rest = {}, list(scratch)
    for name in NAMES:
        bufs[name] = [rest.pop(0) for _ in CHUNKS]
    w, acc, cot1, cot, act, act1, send, recv = rest
    dev = Device()
    core, at = dev.core, dev.at
    x, y, z = at["x"], at["y"], at["z"]
    half = x // 2
    m = Moves(dev, send, recv)
    plane = [(dz, dh) for dz in range(4) for dh in range(2) if (dz, dh) != (0, 0)]

    def in_plane(dz, dh):
        return dict(z=(z + dz) % RING, x=((half + dh) % 2) * 2 + x % 2)

    w_sem, own_sems = m.sem(), [m.sem() for _ in CHUNKS]
    for c in range(2):
        for lo in range(2):
            m.here(w_ref.at[lo, c], w.at[c, pl.ds(lo * FEAT, FEAT)], w_sem)
    own_blocks = [bufs["x"][k].at[core, z, half, :, :, cols(x)] for k in CHUNKS]
    for k in CHUNKS:
        m.here(in_ref.at[:, pl.ds(STARTS[k], SPANS[k])], own_blocks[k], own_sems[k])

    barrier = pltpu.get_barrier_semaphore()
    peers = [dict(core=1 - core), dict(x=dev.along("x", 1)), dict(x=dev.along("x", 3))]
    peers += [dict(y=dev.along("y", s)) for s in (1, 2, 3)] + [in_plane(*step) for step in plane if 0 in step]
    for peer in peers:
        pl.semaphore_signal(barrier, inc=1, device_id=dev.name(**peer), device_id_type=MESH)
    pl.semaphore_wait(barrier, len(peers))

    tasks = {}

    def task(name):
        def keep(step):
            tasks[name] = step
            return step

        return keep

    landed, core_sems = set(), []

    def input_tasks(k):
        b = bufs["x"][k]
        rows = pl.ds(STARTS[k], SPANS[k])

        ax = Straight(m, "x", b.at[core, pl.ds(0, 3), 0, pl.ds(0, 2), :, pl.ds(0, FEAT)])
        az = Straight(m, "z", b.at[core, pl.ds(0, 3), :, pl.ds(0, 2)])
        bz = Straight(m, "z", b.at[core, pl.ds(0, 3), 0, pl.ds(0, 2), :, pl.ds(0, FEAT)])
        bx = Straight(m, "x", b.at[core, pl.ds(0, 3), 0])
        core_sems.append(m.sem())

        @task(("ax0", k))
        def _():
            ax.send(lambda to: in_ref.at[0:2, rows], lambda step: b.at[core, z, half, 0:2, :, cols(x)])

        @task(("bz0", k))
        def _():
            bz.send(lambda to: in_ref.at[2:4, rows], lambda step: b.at[core, z, half, 2:4, :, cols(x)])

        def own_landed():
            if k not in landed:
                m.wait(own_blocks[k], own_sems[k])
                landed.add(k)

        @task(("ax2", k))
        def _():
            own_landed()
            ax.arrive()
            view = b.at[core, z, :, 0:2]
            az.send(lambda to: view, lambda step: view)

        @task(("bz2", k))
        def _():
            own_landed()
            bz.arrive()
            view = b.at[core, :, half, 2:4, :, cols(x)]
            bx.send(lambda to: view, lambda step: view)

        def give(ring, first_row):
            ring.arrive()
            view = b.at[core, :, :, pl.ds(first_row, 2)]
            m.start(view, view, core_sems[k], core=1 - core)

        tasks["az2", k] = lambda: give(az, 0)
        tasks["bx2", k] = lambda: give(bx, 2)

    for k in CHUNKS:
        input_tasks(k)

    def rows_of(part):
        first, end = part
        return pl.ds(STARTS[first], sum(SPANS[first:end]))

    def cot_tasks(i):
        rows, y_sem, plane_sem = rows_of(COT_PARTS[i]), m.sem(), m.sem()

        @task(("c0", i))
        def _():
            m.here(cot_ref.at[y, rows], cot1.at[y, rows], y_sem)
            for s in (1, 2, 3):
                to = dev.along("y", s)
                m.start(cot_ref.at[to, rows], cot1.at[y, rows], y_sem, y=to)

        @task(("c1", i))
        def _():
            m.wait(cot1.at[:, rows], y_sem)

            def source(to):
                return cot1.at[to["z"], rows, pl.ds(pl.multiple_of((to["x"] // 2) * HID, HID), HID)]

            dst = cot.at[z, half, rows]
            m.here(source(at), dst, plane_sem)
            for to in others:
                m.start(source(to), dst, plane_sem, **to)

        def landed():
            m.wait(cot.at[:, :, rows], plane_sem)

        return landed

    others = [in_plane(*step) for step in plane]
    cot_landed = [cot_tasks(i) for i in range(len(COT_PARTS))]

    def act_tasks(i):
        rows, plane_sem, y_sem = rows_of(ACT_PARTS[i]), m.sem(), m.sem()

        @task(("p0", i))
        def _():
            dst = act1.at[z, rows, pl.ds(pl.multiple_of(half * HID, HID), HID)]
            m.here(act.at[z, half, rows], dst, plane_sem)
            for to in others:
                m.start(act.at[to["z"], to["x"] // 2, rows], dst, plane_sem, **to)

        @task(("p1", i))
        def _():
            m.wait(act1.at[:, rows], plane_sem)
            m.here(act1.at[y, rows], act_ref.at[y, rows], y_sem)
            for s in (1, 2, 3):
                to = dev.along("y", s)
                m.start(act1.at[to, rows], act_ref.at[y, rows], y_sem, y=to)

        tasks["p2", i] = lambda: m.wait(act_ref.at[:, rows], y_sem)

    for i in range(len(ACT_PARTS)):
        act_tasks(i)

    def main_tasks(k):
        b, p, s, d, near = (bufs[name][k] for name in ("x", "p", "s", "d", "ynear"))
        r, rows = SPANS[k], pl.ds(STARTS[k], SPANS[k])
        total = Reduce(m, "y", lambda q, part: p.at[pl.ds(2 * part, 2), :, q], bufs["yfar"][k], near)
        spread = Gather(m, "y", lambda q, part: s.at[pl.ds(2 * part, 2), :, q], s.at[:, :, 0:2])
        cross_sem = m.sem()

        @task(("P", k))
        def _():
            m.wait(b.at[1 - core], core_sems[k])
            if "w" not in landed:
                m.wait(w, w_sem)
                landed.add("w")

            def tile(n, carry):
                where = pl.ds(pl.multiple_of(n * 256, 256), 256)
                value = jnp.dot(b[0].reshape(32 * r, HID), w[0, :, where], preferred_element_type=F32)
                value += jnp.dot(b[1].reshape(32 * r, HID), w[1, :, where], preferred_element_type=F32)
                p[:, :, :, :, where] = value.astype(BF16).reshape(4, 2, 4, r, 256)
                return carry

            lax.fori_loop(0, 3, tile, 0)
            total.begin()

        tasks["R1a", k], tasks["R1b", k] = total.middle_up, total.middle_down

        @task(("G", k))
        def _():
            total.arrive()
            for i, (first, end) in enumerate(COT_PARTS):
                if first <= k < end and ("cot", i) not in landed:
                    cot_landed[i]()
                    landed.add(("cot", i))

            def step(i, carry):
                zz, hh = i // 2, i % 2
                value = p[zz, hh, y].astype(F32)
                value = value + near[0, zz // 2, zz % 2, hh].astype(F32) + near[1, zz // 2, zz % 2, hh].astype(F32)
                a, slope = gelu_and_slope(value, cot[zz, hh, rows].astype(F32))
                act[zz, hh, rows] = a.astype(BF16)
                s[zz, hh, y] = slope.astype(BF16)
                return carry

            lax.fori_loop(0, 8, step, 0)
            spread.begin()

        tasks["A1a", k], tasks["A1b", k] = spread.forward_up, spread.forward_down

        def input_terms(c):
            def tile(n, carry):
                where = pl.ds(pl.multiple_of(n * 256, 256), 256)
                value = lax.dot_general(
                    s[...].reshape(32 * r, HID), w[c, where, :], (((1,), (1,)), ((), ())), preferred_element_type=F32
                )
                d[c, :, :, :, :, where] = value.astype(BF16).reshape(4, 2, 4, r, 256)
                return carry

            lax.fori_loop(0, 3, tile, 0)

        @task(("Dh", k))
        def _():
            spread.end()
            input_terms(1 - core)
            m.start(d.at[1 - core], bufs["core"][k], cross_sem, core=1 - core)

        @task(("Dl", k))
        def _():
            input_terms(core)

        @task(("W", k))
        def _():
            def tile(n, carry):
                c = n // 3
                where = pl.ds(pl.multiple_of((n % 3) * 256, 256), 256)
                value = lax.dot_general(
                    b[c, :, :, :, :, where].reshape(32 * r, 256), s[...].reshape(32 * r, HID),
                    (((0,), (0,)), ((), ())), preferred_element_type=F32,
                )
                if k > 0:
                    value = value + acc[c, where, :]
                if k < last:
                    acc[c, where, :] = value
                else:
                    dw_ref[c, where, :] = value.astype(BF16)
                return carry

            lax.fori_loop(0, 6, tile, 0)

        ax, az, bz, bx = (Straight(m, axis, bufs[name][k]) for name, axis in (("ax", "x"), ("az", "z"), ("bz", "z"), ("bx", "x")))
        land = {name: bufs[name][k] for name in ("ax", "az", "bz", "bx")}

        def pieces(name):
            return {
                "ax": lambda q: d.at[core, :, q // 2, 0:2, :, cols(q)],
                "bz": lambda q: d.at[core, q, :, 2:4],
                "az": lambda q: d.at[core, q, half, 0:2, :, cols(x)],
                "bx": lambda q: d.at[core, z, q // 2, 2:4, :, cols(q)],
            }[name]

        def send(ring, name):
            ring.send(pieces(name), lambda step: land[name].at[step - 1])

        def finish(ring, name):
            ring.arrive()
            add_rows(pieces(name)(at[ring.axis]), *(land[name].at[i] for i in range(3)))

        @task(("dx0", k))
        def _():
            m.wait(bufs["core"][k], cross_sem)
            add_rows(d.at[core], bufs["core"][k])
            send(ax, "ax")
            send(bz, "bz")

        @task(("rx2", k))
        def _():
            finish(ax, "ax")
            send(az, "az")

        @task(("rz2", k))
        def _():
            finish(bz, "bz")
            send(bx, "bx")

        @task(("sz2", k))
        def _():
            finish(az, "az")
            dx_ref[0:2, rows, :] = d[core, z, half, 0:2, :, cols(x)]

        @task(("sx2", k))
        def _():
            finish(bx, "bx")
            dx_ref[2:4, rows, :] = d[core, z, half, 2:4, :, cols(x)]

    last = len(SPANS) - 1
    for k in CHUNKS:
        main_tasks(k)
    for step in ORDER:
        tasks[step]()
    m.drain()


def on_device(inputs, weight, cotangent):
    shapes = [pltpu.VMEM(shape, BF16) for name, each in scratch_of().items() for shape in each]
    act, dx, dw = pl.pallas_call(
        kernel,
        out_shape=(
            pltpu.VMEM((4, OWN, 2 * HID), BF16),
            pltpu.VMEM((4, OWN, FEAT), BF16),
            pltpu.VMEM((2, HID, HID), BF16),
        ),
        in_specs=[
            pl.BlockSpec(memory_space=pltpu.VMEM),
            pl.BlockSpec(memory_space=pl.ANY),
            pl.BlockSpec(memory_space=pl.ANY),
        ],
        out_specs=(
            pl.BlockSpec(memory_space=pltpu.VMEM),
            pl.BlockSpec(memory_space=pltpu.VMEM),
            pl.BlockSpec(memory_space=pltpu.VMEM),
        ),
        scratch_shapes=[
            *shapes,
            pltpu.VMEM((2, HID, HID), BF16),
            pltpu.VMEM((2, HID, HID), F32),
            pltpu.VMEM((4, OWN, 2 * HID), BF16),
            pltpu.VMEM((4, 2, OWN, HID), BF16),
            pltpu.VMEM((4, 2, OWN, HID), BF16),
            pltpu.VMEM((4, OWN, 2 * HID), BF16),
            pltpu.SemaphoreType.DMA,
            pltpu.SemaphoreType.DMA((N_SEM,)),
        ],
        compiler_params=pltpu.CompilerParams(
            collective_id=0, has_side_effects=True, vmem_limit_bytes=58 * 2**20
        ),
        cost_estimate=pl.CostEstimate(flops=6 * 384 * 1536 * 6144, bytes_accessed=8 * 2**20, transcendentals=0),
    )(
        inputs.reshape(4, OWN, FEAT),
        weight.reshape(2, 2, FEAT, HID),
        cotangent.reshape(4, OWN, 2 * HID),
    )

    def write_out(act_ref, dx_ref, dw_ref, act_out, dx_out, dw_out, sems):
        pairs = [(act_ref, act_out), (dx_ref, dx_out)]
        pairs += [(dw_ref.at[c, pl.ds(lo * FEAT, FEAT)], dw_out.at[lo, c]) for c in range(2) for lo in range(2)]
        copies = [pltpu.make_async_copy(src, dst, sems.at[i]) for i, (src, dst) in enumerate(pairs)]
        for copy in copies:
            copy.start()
        for copy in copies:
            copy.wait()

    act, dx, dw = pl.pallas_call(
        write_out,
        out_shape=(
            jax.ShapeDtypeStruct((4, OWN, 2 * HID), BF16),
            jax.ShapeDtypeStruct((4, OWN, FEAT), BF16),
            jax.ShapeDtypeStruct((2, 2, FEAT, HID), BF16),
        ),
        in_specs=[pl.BlockSpec(memory_space=pl.ANY)] * 3,
        out_specs=(pl.BlockSpec(memory_space=pl.ANY),) * 3,
        scratch_shapes=[pltpu.SemaphoreType.DMA((6,))],
        compiler_params=pltpu.CompilerParams(vmem_limit_bytes=2**20),
    )(act, dx, dw)
    return act.reshape(4 * OWN, 2 * HID), dx.reshape(4 * OWN, FEAT), dw.reshape(4 * FEAT, HID)


def solution(mesh):
    return jax.shard_map(
        on_device,
        mesh=mesh,
        in_specs=(P("gy", ("gz", "gx")), P("gz", ("gx", "gy")), P("gy", ("gx", "gz"))),
        out_specs=(P("gy", ("gx", "gz")), P("gy", ("gz", "gx")), P("gz", ("gx", "gy"))),
        check_vma=False,
    )
```

```python
import functools

import jax
import jax.numpy as jnp
from jax import lax
from jax.experimental import pallas as pl
from jax.experimental.pallas import tpu as pltpu
from jax.sharding import PartitionSpec as P

MESH = pl.DeviceIdType.MESH
F32, BF16 = jnp.float32, jnp.bfloat16
RING = 4
SPANS = (16, 16, 16, 16, 16, 16)
OWN = sum(SPANS)
STARTS = tuple(sum(SPANS[:k]) for k in range(len(SPANS)))
CHUNKS = range(len(SPANS))
HID = 768
FEAT = 384
COT_PARTS = ((0, 1), (1, 6))
ACT_PARTS = ((0, 5), (5, 6))
N_SEM = 17 * len(SPANS) + 2 * (len(COT_PARTS) + len(ACT_PARTS)) + 2
ORDER = (
    ("bz0", 0), ("c0", 0), ("ax0", 0), ("ax0", 2), ("bz0", 2), ("ax0", 1), ("bz0", 3), ("bz0", 1), ("bz2", 0),
    ("c0", 1), ("ax2", 0), ("ax2", 1), ("bz0", 4), ("bz2", 1), ("ax0", 4), ("ax2", 2), ("ax0", 3), ("bx2", 0),
    ("bz2", 2), ("az2", 0), ("c1", 0), ("P", 0), ("bx2", 1), ("az2", 1), ("P", 1), ("az2", 2), ("bz2", 3),
    ("bz2", 4), ("bz0", 5), ("bx2", 2), ("R1a", 0), ("ax2", 4), ("ax2", 3), ("ax0", 5), ("R1b", 0), ("P", 2),
    ("R1a", 1), ("G", 0), ("bx2", 3), ("c1", 1), ("R1a", 2), ("az2", 4), ("R1b", 1), ("az2", 3), ("bx2", 4),
    ("R1b", 2), ("P", 3), ("P", 4), ("ax2", 5), ("A1b", 0), ("A1a", 0), ("R1a", 3), ("bz2", 5), ("G", 2),
    ("R1b", 4), ("R1a", 4), ("G", 1), ("R1b", 3), ("Dh", 0), ("bx2", 5), ("A1b", 2), ("az2", 5), ("Dl", 0),
    ("dx0", 0), ("P", 5), ("A1a", 2), ("W", 0), ("A1b", 1), ("A1a", 1), ("G", 4), ("G", 3), ("p0", 0),
    ("rx2", 0), ("Dh", 2), ("Dh", 1), ("W", 1), ("R1a", 5), ("R1b", 5), ("Dl", 2), ("dx0", 2), ("rz2", 0),
    ("A1b", 3), ("A1a", 3), ("Dl", 1), ("sz2", 0), ("A1a", 4), ("dx0", 1), ("A1b", 4), ("W", 2), ("G", 5),
    ("p0", 1), ("Dh", 3), ("W", 3), ("Dl", 3), ("dx0", 3), ("A1b", 5), ("A1a", 5), ("p1", 0), ("Dh", 4),
    ("Dl", 4), ("rx2", 1), ("rz2", 1), ("dx0", 4), ("Dh", 5), ("sx2", 0), ("Dl", 5), ("dx0", 5), ("rz2", 3),
    ("p1", 1), ("rx2", 2), ("rx2", 3), ("W", 4), ("rz2", 2), ("rz2", 4), ("W", 5), ("rx2", 4), ("rz2", 5),
    ("rx2", 5), ("sz2", 1), ("p2", 0), ("sz2", 3), ("p2", 1), ("sx2", 1), ("sx2", 3), ("sx2", 4), ("sx2", 2),
    ("sz2", 2), ("sz2", 4), ("sx2", 5), ("sz2", 5),
)


class Device:
    def __init__(self):
        gx, gy, gz = (lax.axis_index(name) for name in ("gx", "gy", "gz"))
        self.core = gx % 2
        self.at = {"x": (gy % 2) * 2 + gx // 2, "y": gz, "z": gy // 2}

    def name(self, core=None, **at):
        at = {**self.at, **at}
        core = self.core if core is None else core
        return {"gx": (at["x"] % 2) * 2 + core, "gy": at["z"] * 2 + at["x"] // 2, "gz": at["y"]}

    def along(self, axis, step):
        return (self.at[axis] + step) % RING


def cols(x):
    return pl.ds(pl.multiple_of((x % 2) * FEAT, FEAT), FEAT)


def gelu_and_slope(value, cotangent):
    scale, cubic = 0.7978845608028654, 0.044715
    square = value * value
    t = jnp.tanh(scale * value * (1.0 + cubic * square))
    half = 0.5 * (1.0 + t)
    slope = half + 0.5 * value * ((1.0 + t) * (1.0 - t)) * (scale + (3.0 * cubic * scale) * square)
    return value * half, cotangent * slope


def add_into(dst, *srcs):
    total = dst[...].astype(F32)
    for src in srcs:
        total = total + src[...].astype(F32)
    dst[...] = total.astype(BF16)


def add_rows(dst, *srcs):
    def step(i, carry):
        add_into(dst.at[i], *(src.at[i] for src in srcs))
        return carry

    lax.fori_loop(0, dst.shape[0], step, 0)


class Moves:
    def __init__(self, device, send, recv):
        self.device, self.send, self.recv = device, send, recv
        self.count = 0
        self.sent = []

    def sem(self):
        self.count += 1
        return self.recv.at[self.count - 1]

    def start(self, src, dst, sem, **to):
        copy = pltpu.make_async_remote_copy(
            src_ref=src, dst_ref=dst, send_sem=self.send, recv_sem=sem,
            device_id=self.device.name(**to), device_id_type=MESH,
        )
        copy.start()
        self.sent.append(copy)

    def here(self, src, dst, sem):
        pltpu.make_async_copy(src, dst, sem).start()

    def wait(self, size, sem):
        pltpu.make_async_copy(size, size, sem).wait()

    def drain(self):
        for copy in self.sent:
            copy.wait_send()
        self.sent = []


class Straight:
    def __init__(self, moves, axis, size):
        self.m, self.axis, self.size, self.sem = moves, axis, size, moves.sem()

    def send(self, src, dst):
        for step in (1, 3, 2):
            to = self.m.device.along(self.axis, step)
            self.m.start(src(to), dst(step), self.sem, **{self.axis: to})

    def arrive(self):
        self.m.wait(self.size, self.sem)


class Gather:
    def __init__(self, moves, axis, slot, rest):
        self.m, self.axis, self.slot, self.rest = moves, axis, slot, rest
        self.up_sem, self.down_sem, self.rest_sem = moves.sem(), moves.sem(), moves.sem()

    def begin(self):
        d, a = self.m.device, self.axis
        me, up, down = d.at[a], {a: d.along(a, 1)}, {a: d.along(a, 3)}
        first, second = self.slot(me, 0), self.slot(me, 1)
        self.m.start(first, first, self.up_sem, **up)
        self.m.start(second, second, self.down_sem, **down)
        self.m.start(second, second, self.rest_sem, **up)
        self.m.start(first, first, self.rest_sem, **down)

    def forward_up(self):
        d, a = self.m.device, self.axis
        view = self.slot(d.along(a, 3), 0)
        self.m.wait(view, self.up_sem)
        self.m.start(view, view, self.rest_sem, **{a: d.along(a, 1)})

    def forward_down(self):
        d, a = self.m.device, self.axis
        view = self.slot(d.along(a, 1), 1)
        self.m.wait(view, self.down_sem)
        self.m.start(view, view, self.rest_sem, **{a: d.along(a, 3)})

    def end(self):
        self.m.wait(self.rest, self.rest_sem)


class Reduce:
    def __init__(self, moves, axis, piece, far, near):
        self.m, self.axis, self.piece, self.far, self.near = moves, axis, piece, far, near
        self.up_sem, self.down_sem, self.near_sem = moves.sem(), moves.sem(), moves.sem()

    def begin(self):
        d, a, p = self.m.device, self.axis, self.piece
        up, down, across = d.along(a, 1), d.along(a, 3), d.along(a, 2)
        self.m.start(p(across, 0), self.far.at[0], self.up_sem, **{a: up})
        self.m.start(p(across, 1), self.far.at[1], self.down_sem, **{a: down})
        self.m.start(p(up, 1), self.near.at[0, 1], self.near_sem, **{a: up})
        self.m.start(p(down, 0), self.near.at[1, 0], self.near_sem, **{a: down})

    def middle_up(self):
        d, a = self.m.device, self.axis
        up = d.along(a, 1)
        self.m.wait(self.far.at[0], self.up_sem)
        add_rows(self.piece(up, 0), self.far.at[0])
        self.m.start(self.piece(up, 0), self.near.at[0, 0], self.near_sem, **{a: up})

    def middle_down(self):
        d, a = self.m.device, self.axis
        down = d.along(a, 3)
        self.m.wait(self.far.at[1], self.down_sem)
        add_rows(self.piece(down, 1), self.far.at[1])
        self.m.start(self.piece(down, 1), self.near.at[1, 1], self.near_sem, **{a: down})

    def arrive(self):
        self.m.wait(self.near, self.near_sem)


def scratch_of():
    shapes = {}
    for k in CHUNKS:
        r = SPANS[k]
        block = (4, 2, 4, r, HID)
        for name, shape in dict(
            x=(2, *block), p=block, s=block, d=(2, *block), core=block,
            yfar=(2, 2, 2, r, HID), ynear=(2, 2, 2, 2, r, HID),
            ax=(3, 4, 2, r, FEAT), az=(3, 2, r, FEAT), bz=(3, 2, 2, r, HID), bx=(3, 2, r, FEAT),
        ).items():
            shapes.setdefault(name, []).append(shape)
    return shapes


NAMES = tuple(scratch_of())


def kernel(in_ref, w_ref, cot_ref, act_ref, dx_ref, dw_ref, *scratch):
    bufs, rest = {}, list(scratch)
    for name in NAMES:
        bufs[name] = [rest.pop(0) for _ in CHUNKS]
    w, acc, cot1, cot, act, act1, send, recv = rest
    dev = Device()
    core, at = dev.core, dev.at
    x, y, z = at["x"], at["y"], at["z"]
    half = x // 2
    m = Moves(dev, send, recv)
    plane = [(dz, dh) for dz in range(4) for dh in range(2) if (dz, dh) != (0, 0)]

    def in_plane(dz, dh):
        return dict(z=(z + dz) % RING, x=((half + dh) % 2) * 2 + x % 2)

    w_sem, own_sems = m.sem(), [m.sem() for _ in CHUNKS]
    for c in range(2):
        for lo in range(2):
            m.here(w_ref.at[lo, c], w.at[c, pl.ds(lo * FEAT, FEAT)], w_sem)
    own_blocks = [bufs["x"][k].at[core, z, half, :, :, cols(x)] for k in CHUNKS]
    for k in CHUNKS:
        m.here(in_ref.at[:, pl.ds(STARTS[k], SPANS[k])], own_blocks[k], own_sems[k])

    barrier = pltpu.get_barrier_semaphore()
    peers = [dict(core=1 - core), dict(x=dev.along("x", 1)), dict(x=dev.along("x", 3))]
    peers += [dict(y=dev.along("y", s)) for s in (1, 2, 3)] + [in_plane(*step) for step in plane if 0 in step]
    for peer in peers:
        pl.semaphore_signal(barrier, inc=1, device_id=dev.name(**peer), device_id_type=MESH)
    pl.semaphore_wait(barrier, len(peers))

    tasks = {}

    def task(name):
        def keep(step):
            tasks[name] = step
            return step

        return keep

    landed, core_sems = set(), []

    def input_tasks(k):
        b = bufs["x"][k]
        rows = pl.ds(STARTS[k], SPANS[k])

        ax = Straight(m, "x", b.at[core, pl.ds(0, 3), 0, pl.ds(0, 2), :, pl.ds(0, FEAT)])
        az = Straight(m, "z", b.at[core, pl.ds(0, 3), :, pl.ds(0, 2)])
        bz = Straight(m, "z", b.at[core, pl.ds(0, 3), 0, pl.ds(0, 2), :, pl.ds(0, FEAT)])
        bx = Straight(m, "x", b.at[core, pl.ds(0, 3), 0])
        core_sems.append(m.sem())

        @task(("ax0", k))
        def _():
            ax.send(lambda to: in_ref.at[0:2, rows], lambda step: b.at[core, z, half, 0:2, :, cols(x)])

        @task(("bz0", k))
        def _():
            bz.send(lambda to: in_ref.at[2:4, rows], lambda step: b.at[core, z, half, 2:4, :, cols(x)])

        def own_landed():
            if k not in landed:
                m.wait(own_blocks[k], own_sems[k])
                landed.add(k)

        @task(("ax2", k))
        def _():
            own_landed()
            ax.arrive()
            view = b.at[core, z, :, 0:2]
            az.send(lambda to: view, lambda step: view)

        @task(("bz2", k))
        def _():
            own_landed()
            bz.arrive()
            view = b.at[core, :, half, 2:4, :, cols(x)]
            bx.send(lambda to: view, lambda step: view)

        def give(ring, first_row):
            ring.arrive()
            view = b.at[core, :, :, pl.ds(first_row, 2)]
            m.start(view, view, core_sems[k], core=1 - core)

        tasks["az2", k] = lambda: give(az, 0)
        tasks["bx2", k] = lambda: give(bx, 2)

    for k in CHUNKS:
        input_tasks(k)

    def rows_of(part):
        first, end = part
        return pl.ds(STARTS[first], sum(SPANS[first:end]))

    def cot_tasks(i):
        rows, y_sem, plane_sem = rows_of(COT_PARTS[i]), m.sem(), m.sem()

        @task(("c0", i))
        def _():
            m.here(cot_ref.at[y, rows], cot1.at[y, rows], y_sem)
            for s in (1, 2, 3):
                to = dev.along("y", s)
                m.start(cot_ref.at[to, rows], cot1.at[y, rows], y_sem, y=to)

        @task(("c1", i))
        def _():
            m.wait(cot1.at[:, rows], y_sem)

            def source(to):
                return cot1.at[to["z"], rows, pl.ds(pl.multiple_of((to["x"] // 2) * HID, HID), HID)]

            dst = cot.at[z, half, rows]
            m.here(source(at), dst, plane_sem)
            for to in others:
                m.start(source(to), dst, plane_sem, **to)

        def landed():
            m.wait(cot.at[:, :, rows], plane_sem)

        return landed

    others = [in_plane(*step) for step in plane]
    cot_landed = [cot_tasks(i) for i in range(len(COT_PARTS))]

    def act_tasks(i):
        rows, plane_sem, y_sem = rows_of(ACT_PARTS[i]), m.sem(), m.sem()

        @task(("p0", i))
        def _():
            dst = act1.at[z, rows, pl.ds(pl.multiple_of(half * HID, HID), HID)]
            m.here(act.at[z, half, rows], dst, plane_sem)
            for to in others:
                m.start(act.at[to["z"], to["x"] // 2, rows], dst, plane_sem, **to)

        @task(("p1", i))
        def _():
            m.wait(act1.at[:, rows], plane_sem)
            m.here(act1.at[y, rows], act_ref.at[y, rows], y_sem)
            for s in (1, 2, 3):
                to = dev.along("y", s)
                m.start(act1.at[to, rows], act_ref.at[y, rows], y_sem, y=to)

        tasks["p2", i] = lambda: m.wait(act_ref.at[:, rows], y_sem)

    for i in range(len(ACT_PARTS)):
        act_tasks(i)

    def main_tasks(k):
        b, p, s, d, near = (bufs[name][k] for name in ("x", "p", "s", "d", "ynear"))
        r, rows = SPANS[k], pl.ds(STARTS[k], SPANS[k])
        total = Reduce(m, "y", lambda q, part: p.at[pl.ds(2 * part, 2), :, q], bufs["yfar"][k], near)
        spread = Gather(m, "y", lambda q, part: s.at[pl.ds(2 * part, 2), :, q], s.at[:, :, 0:2])
        cross_sem = m.sem()

        @task(("P", k))
        def _():
            m.wait(b.at[1 - core], core_sems[k])
            if "w" not in landed:
                m.wait(w, w_sem)
                landed.add("w")

            value = jnp.dot(b[0].reshape(32 * r, HID), w[0], preferred_element_type=F32)
            value += jnp.dot(b[1].reshape(32 * r, HID), w[1], preferred_element_type=F32)
            p[...] = value.astype(BF16).reshape(4, 2, 4, r, HID)
            total.begin()

        tasks["R1a", k], tasks["R1b", k] = total.middle_up, total.middle_down

        @task(("G", k))
        def _():
            total.arrive()
            for i, (first, end) in enumerate(COT_PARTS):
                if first <= k < end and ("cot", i) not in landed:
                    cot_landed[i]()
                    landed.add(("cot", i))

            def step(i, carry):
                zz, hh = i // 2, i % 2
                value = p[zz, hh, y].astype(F32)
                value = value + near[0, zz // 2, zz % 2, hh].astype(F32) + near[1, zz // 2, zz % 2, hh].astype(F32)
                a, slope = gelu_and_slope(value, cot[zz, hh, rows].astype(F32))
                act[zz, hh, rows] = a.astype(BF16)
                s[zz, hh, y] = slope.astype(BF16)
                return carry

            lax.fori_loop(0, 8, step, 0)
            spread.begin()

        tasks["A1a", k], tasks["A1b", k] = spread.forward_up, spread.forward_down

        def input_terms(c):
            value = lax.dot_general(
                s[...].reshape(32 * r, HID), w[c], (((1,), (1,)), ((), ())), preferred_element_type=F32
            )
            d[c] = value.astype(BF16).reshape(4, 2, 4, r, HID)

        @task(("Dh", k))
        def _():
            spread.end()
            input_terms(1 - core)
            m.start(d.at[1 - core], bufs["core"][k], cross_sem, core=1 - core)

        @task(("Dl", k))
        def _():
            input_terms(core)

        @task(("W", k))
        def _():
            def tile(c, carry):
                value = lax.dot_general(
                    b[c].reshape(32 * r, HID), s[...].reshape(32 * r, HID),
                    (((0,), (0,)), ((), ())), preferred_element_type=F32,
                )
                if k > 0:
                    value = value + acc[c]
                if k < last:
                    acc[c] = value
                else:
                    dw_ref[c] = value.astype(BF16)
                return carry

            lax.fori_loop(0, 2, tile, 0)

        ax, az, bz, bx = (Straight(m, axis, bufs[name][k]) for name, axis in (("ax", "x"), ("az", "z"), ("bz", "z"), ("bx", "x")))
        land = {name: bufs[name][k] for name in ("ax", "az", "bz", "bx")}

        def pieces(name):
            return {
                "ax": lambda q: d.at[core, :, q // 2, 0:2, :, cols(q)],
                "bz": lambda q: d.at[core, q, :, 2:4],
                "az": lambda q: d.at[core, q, half, 0:2, :, cols(x)],
                "bx": lambda q: d.at[core, z, q // 2, 2:4, :, cols(q)],
            }[name]

        def send(ring, name):
            ring.send(pieces(name), lambda step: land[name].at[step - 1])

        def finish(ring, name):
            ring.arrive()
            add_rows(pieces(name)(at[ring.axis]), *(land[name].at[i] for i in range(3)))

        @task(("dx0", k))
        def _():
            m.wait(bufs["core"][k], cross_sem)
            add_rows(d.at[core], bufs["core"][k])
            send(ax, "ax")
            send(bz, "bz")

        @task(("rx2", k))
        def _():
            finish(ax, "ax")
            send(az, "az")

        @task(("rz2", k))
        def _():
            finish(bz, "bz")
            send(bx, "bx")

        @task(("sz2", k))
        def _():
            finish(az, "az")
            dx_ref[0:2, rows, :] = d[core, z, half, 0:2, :, cols(x)]

        @task(("sx2", k))
        def _():
            finish(bx, "bx")
            dx_ref[2:4, rows, :] = d[core, z, half, 2:4, :, cols(x)]

    last = len(SPANS) - 1
    for k in CHUNKS:
        main_tasks(k)
    for step in ORDER:
        tasks[step]()
    m.drain()


def on_device(inputs, weight, cotangent):
    shapes = [pltpu.VMEM(shape, BF16) for name, each in scratch_of().items() for shape in each]
    act, dx, dw = pl.pallas_call(
        kernel,
        out_shape=(
            pltpu.VMEM((4, OWN, 2 * HID), BF16),
            pltpu.VMEM((4, OWN, FEAT), BF16),
            pltpu.VMEM((2, HID, HID), BF16),
        ),
        in_specs=[
            pl.BlockSpec(memory_space=pltpu.VMEM),
            pl.BlockSpec(memory_space=pl.ANY),
            pl.BlockSpec(memory_space=pl.ANY),
        ],
        out_specs=(
            pl.BlockSpec(memory_space=pltpu.VMEM),
            pl.BlockSpec(memory_space=pltpu.VMEM),
            pl.BlockSpec(memory_space=pltpu.VMEM),
        ),
        scratch_shapes=[
            *shapes,
            pltpu.VMEM((2, HID, HID), BF16),
            pltpu.VMEM((2, HID, HID), F32),
            pltpu.VMEM((4, OWN, 2 * HID), BF16),
            pltpu.VMEM((4, 2, OWN, HID), BF16),
            pltpu.VMEM((4, 2, OWN, HID), BF16),
            pltpu.VMEM((4, OWN, 2 * HID), BF16),
            pltpu.SemaphoreType.DMA,
            pltpu.SemaphoreType.DMA((N_SEM,)),
        ],
        compiler_params=pltpu.CompilerParams(
            collective_id=0, has_side_effects=True, vmem_limit_bytes=58 * 2**20
        ),
        cost_estimate=pl.CostEstimate(flops=6 * 384 * 1536 * 6144, bytes_accessed=8 * 2**20, transcendentals=0),
    )(
        inputs.reshape(4, OWN, FEAT),
        weight.reshape(2, 2, FEAT, HID),
        cotangent.reshape(4, OWN, 2 * HID),
    )

    def write_out(act_ref, dx_ref, dw_ref, act_out, dx_out, dw_out, sems):
        pairs = [(act_ref, act_out), (dx_ref, dx_out)]
        pairs += [(dw_ref.at[c, pl.ds(lo * FEAT, FEAT)], dw_out.at[lo, c]) for c in range(2) for lo in range(2)]
        copies = [pltpu.make_async_copy(src, dst, sems.at[i]) for i, (src, dst) in enumerate(pairs)]
        for copy in copies:
            copy.start()
        for copy in copies:
            copy.wait()

    act, dx, dw = pl.pallas_call(
        write_out,
        out_shape=(
            jax.ShapeDtypeStruct((4, OWN, 2 * HID), BF16),
            jax.ShapeDtypeStruct((4, OWN, FEAT), BF16),
            jax.ShapeDtypeStruct((2, 2, FEAT, HID), BF16),
        ),
        in_specs=[pl.BlockSpec(memory_space=pl.ANY)] * 3,
        out_specs=(pl.BlockSpec(memory_space=pl.ANY),) * 3,
        scratch_shapes=[pltpu.SemaphoreType.DMA((6,))],
        compiler_params=pltpu.CompilerParams(vmem_limit_bytes=2**20),
    )(act, dx, dw)
    return act.reshape(4 * OWN, 2 * HID), dx.reshape(4 * OWN, FEAT), dw.reshape(4 * FEAT, HID)


def solution(mesh):
    return jax.shard_map(
        on_device,
        mesh=mesh,
        in_specs=(P("gy", ("gz", "gx")), P("gz", ("gx", "gy")), P("gy", ("gx", "gz"))),
        out_specs=(P("gy", ("gx", "gz")), P("gy", ("gz", "gx")), P("gz", ("gx", "gy"))),
        check_vma=False,
    )
```

```python
import functools

import jax
import jax.numpy as jnp
from jax import lax
from jax.experimental import pallas as pl
from jax.experimental.pallas import tpu as pltpu
from jax.sharding import PartitionSpec as P

MESH = pl.DeviceIdType.MESH
F32, BF16 = jnp.float32, jnp.bfloat16
RING = 4
STEPS = {1: "u", 3: "d", 2: "a"}
SPANS = (16, 16, 16, 16, 16, 16)
OWN = sum(SPANS)
STARTS = tuple(sum(SPANS[:k]) for k in range(len(SPANS)))
CHUNKS = range(len(SPANS))
HID = 768
FEAT = 384
COT_PARTS = ((0, 1), (1, 6))
ACT_PARTS = ((0, 3), (3, 5), (5, 6))
EAGER_IN = (0,)
EAGER_OUT = (5,)
N_SEM = 17 * len(SPANS) + 2 * (len(COT_PARTS) + len(ACT_PARTS)) + 2 + 6 * len(EAGER_IN) + 8 * len(EAGER_OUT)
ORDER = (
    ("ax0", 0), ("bz0", 0), ("c0", 0), ("bz0", 2), ("ax0", 2), ("ax2u", 0), ("c0", 1), ("bz2d", 0),
    ("ax2a", 0), ("bz2u", 0), ("bz2a", 0), ("ax2d", 0), ("bz0", 4), ("bz2", 2), ("bz0", 3), ("ax0", 4),
    ("bz0", 1), ("ax2", 2), ("ax0", 1), ("az2", 0), ("ax0", 3), ("ax0", 5), ("bx2", 0), ("P", 0), ("c1", 0),
    ("bz0", 5), ("bx2", 2), ("bz2", 3), ("az2", 2), ("ax2", 3), ("bz2", 1), ("ax2", 1), ("bz2", 4),
    ("R1a", 0), ("R1b", 0), ("P", 2), ("G", 0), ("ax2", 4), ("bx2", 3), ("R1a", 2), ("az2", 3), ("R1b", 2),
    ("P", 3), ("c1", 1), ("bx2", 1), ("az2", 1), ("ax2", 5), ("A1a", 0), ("bx2", 4), ("A1b", 0), ("az2", 4),
    ("P", 1), ("P", 4), ("Dh", 0), ("R1a", 1), ("R1b", 1), ("bz2", 5), ("G", 2), ("G", 1), ("A1b", 2),
    ("az2", 5), ("R1b", 3), ("Dl", 0), ("R1a", 3), ("dx0", 0), ("p0", 0), ("A1a", 2), ("A1a", 1), ("W", 0),
    ("bx2", 5), ("R1a", 4), ("A1b", 1), ("R1b", 4), ("P", 5), ("Dh", 2), ("Dh", 1), ("rz2", 0), ("G", 4),
    ("Dl", 1), ("dx0", 1), ("R1b", 5), ("G", 3), ("A1b", 4), ("p0", 1), ("Dl", 2), ("R1a", 5), ("W", 1),
    ("dx0", 2), ("rx2", 0), ("A1a", 4), ("A1b", 3), ("A1a", 3), ("W", 2), ("G", 5), ("rz2", 1), ("sx2", 0),
    ("p0", 2), ("Dh", 4), ("rz2", 2), ("rx2", 1), ("rx2", 2), ("Dl", 4), ("dx0", 4), ("A1a", 5), ("A1b", 5),
    ("p1", 1), ("Dh", 3), ("sx2", 2), ("sz2", 1), ("Dl", 3), ("dx0", 3), ("Dh", 5), ("p1", 2), ("sz2", 2),
    ("p1", 0), ("Dl", 5), ("dx0", 5), ("W", 3), ("W", 4), ("rx2", 3), ("rz2", 4), ("rx2", 4), ("p2", 2),
    ("rz2", 3), ("rx2a", 5), ("rz2a", 5), ("rz2u", 5), ("sx2", 1), ("rx2u", 5), ("rx2d", 5), ("p2", 1),
    ("sz2", 0), ("rz2d", 5), ("W", 5), ("sx2", 4), ("p2", 0), ("sz2", 3), ("sx2", 3), ("sz2", 4), ("sz2", 5),
    ("sx2", 5),
)


class Device:
    def __init__(self):
        gx, gy, gz = (lax.axis_index(name) for name in ("gx", "gy", "gz"))
        self.core = gx % 2
        self.at = {"x": (gy % 2) * 2 + gx // 2, "y": gz, "z": gy // 2}

    def name(self, core=None, **at):
        at = {**self.at, **at}
        core = self.core if core is None else core
        return {"gx": (at["x"] % 2) * 2 + core, "gy": at["z"] * 2 + at["x"] // 2, "gz": at["y"]}

    def along(self, axis, step):
        return (self.at[axis] + step) % RING


def cols(x):
    return pl.ds(pl.multiple_of((x % 2) * FEAT, FEAT), FEAT)


def gelu_and_slope(value, cotangent):
    scale, cubic = 0.7978845608028654, 0.044715
    square = value * value
    t = jnp.tanh(scale * value * (1.0 + cubic * square))
    half = 0.5 * (1.0 + t)
    slope = half + 0.5 * value * ((1.0 + t) * (1.0 - t)) * (scale + (3.0 * cubic * scale) * square)
    return value * half, cotangent * slope


def add_into(dst, *srcs):
    total = dst[...].astype(F32)
    for src in srcs:
        total = total + src[...].astype(F32)
    dst[...] = total.astype(BF16)


def add_rows(dst, *srcs):
    def step(i, carry):
        add_into(dst.at[i], *(src.at[i] for src in srcs))
        return carry

    lax.fori_loop(0, dst.shape[0], step, 0)


class Moves:
    def __init__(self, device, send, recv):
        self.device, self.send, self.recv = device, send, recv
        self.count = 0
        self.sent = []

    def sem(self):
        self.count += 1
        return self.recv.at[self.count - 1]

    def start(self, src, dst, sem, **to):
        copy = pltpu.make_async_remote_copy(
            src_ref=src, dst_ref=dst, send_sem=self.send, recv_sem=sem,
            device_id=self.device.name(**to), device_id_type=MESH,
        )
        copy.start()
        self.sent.append(copy)

    def here(self, src, dst, sem):
        pltpu.make_async_copy(src, dst, sem).start()

    def wait(self, size, sem):
        pltpu.make_async_copy(size, size, sem).wait()

    def drain(self):
        for copy in self.sent:
            copy.wait_send()
        self.sent = []


class Straight:
    def __init__(self, moves, axis, size):
        self.m, self.axis, self.size, self.sem = moves, axis, size, moves.sem()

    def send(self, src, dst, sems=None):
        for step in STEPS:
            to = self.m.device.along(self.axis, step)
            self.m.start(src(to), dst(step), sems[step] if sems else self.sem, **{self.axis: to})

    def arrive(self):
        self.m.wait(self.size, self.sem)


class Gather:
    def __init__(self, moves, axis, slot, rest):
        self.m, self.axis, self.slot, self.rest = moves, axis, slot, rest
        self.up_sem, self.down_sem, self.rest_sem = moves.sem(), moves.sem(), moves.sem()

    def begin(self):
        d, a = self.m.device, self.axis
        me, up, down = d.at[a], {a: d.along(a, 1)}, {a: d.along(a, 3)}
        first, second = self.slot(me, 0), self.slot(me, 1)
        self.m.start(first, first, self.up_sem, **up)
        self.m.start(second, second, self.down_sem, **down)
        self.m.start(second, second, self.rest_sem, **up)
        self.m.start(first, first, self.rest_sem, **down)

    def forward_up(self):
        d, a = self.m.device, self.axis
        view = self.slot(d.along(a, 3), 0)
        self.m.wait(view, self.up_sem)
        self.m.start(view, view, self.rest_sem, **{a: d.along(a, 1)})

    def forward_down(self):
        d, a = self.m.device, self.axis
        view = self.slot(d.along(a, 1), 1)
        self.m.wait(view, self.down_sem)
        self.m.start(view, view, self.rest_sem, **{a: d.along(a, 3)})

    def end(self):
        self.m.wait(self.rest, self.rest_sem)


class Reduce:
    def __init__(self, moves, axis, piece, far, near):
        self.m, self.axis, self.piece, self.far, self.near = moves, axis, piece, far, near
        self.up_sem, self.down_sem, self.near_sem = moves.sem(), moves.sem(), moves.sem()

    def begin(self):
        d, a, p = self.m.device, self.axis, self.piece
        up, down, across = d.along(a, 1), d.along(a, 3), d.along(a, 2)
        self.m.start(p(across, 0), self.far.at[0], self.up_sem, **{a: up})
        self.m.start(p(across, 1), self.far.at[1], self.down_sem, **{a: down})
        self.m.start(p(up, 1), self.near.at[0, 1], self.near_sem, **{a: up})
        self.m.start(p(down, 0), self.near.at[1, 0], self.near_sem, **{a: down})

    def middle_up(self):
        d, a = self.m.device, self.axis
        up = d.along(a, 1)
        self.m.wait(self.far.at[0], self.up_sem)
        add_rows(self.piece(up, 0), self.far.at[0])
        self.m.start(self.piece(up, 0), self.near.at[0, 0], self.near_sem, **{a: up})

    def middle_down(self):
        d, a = self.m.device, self.axis
        down = d.along(a, 3)
        self.m.wait(self.far.at[1], self.down_sem)
        add_rows(self.piece(down, 1), self.far.at[1])
        self.m.start(self.piece(down, 1), self.near.at[1, 1], self.near_sem, **{a: down})

    def arrive(self):
        self.m.wait(self.near, self.near_sem)


def scratch_of():
    shapes = {}
    for k in CHUNKS:
        r = SPANS[k]
        block = (4, 2, 4, r, HID)
        for name, shape in dict(
            x=(2, *block), p=block, s=block, d=(2, *block), core=block,
            yfar=(2, 2, 2, r, HID), ynear=(2, 2, 2, 2, r, HID),
            ax=(3, 4, 2, r, FEAT), az=(3, 2, r, FEAT), bz=(3, 2, 2, r, HID), bx=(3, 2, r, FEAT),
        ).items():
            shapes.setdefault(name, []).append(shape)
    return shapes


NAMES = tuple(scratch_of())


def kernel(in_ref, w_ref, cot_ref, act_ref, dx_ref, dw_ref, *scratch):
    bufs, rest = {}, list(scratch)
    for name in NAMES:
        bufs[name] = [rest.pop(0) for _ in CHUNKS]
    w, acc, cot1, cot, act, act1, send, recv = rest
    dev = Device()
    core, at = dev.core, dev.at
    x, y, z = at["x"], at["y"], at["z"]
    half = x // 2
    m = Moves(dev, send, recv)
    plane = [(dz, dh) for dz in range(4) for dh in range(2) if (dz, dh) != (0, 0)]

    def in_plane(dz, dh):
        return dict(z=(z + dz) % RING, x=((half + dh) % 2) * 2 + x % 2)

    w_sem, own_sems = m.sem(), [m.sem() for _ in CHUNKS]
    for c in range(2):
        for lo in range(2):
            m.here(w_ref.at[lo, c], w.at[c, pl.ds(lo * FEAT, FEAT)], w_sem)
    own_blocks = [bufs["x"][k].at[core, z, half, :, :, cols(x)] for k in CHUNKS]
    for k in CHUNKS:
        m.here(in_ref.at[:, pl.ds(STARTS[k], SPANS[k])], own_blocks[k], own_sems[k])

    barrier = pltpu.get_barrier_semaphore()
    peers = [dict(core=1 - core), dict(x=dev.along("x", 1)), dict(x=dev.along("x", 3))]
    peers += [dict(y=dev.along("y", s)) for s in (1, 2, 3)] + [in_plane(*step) for step in plane if 0 in step]
    for peer in peers:
        pl.semaphore_signal(barrier, inc=1, device_id=dev.name(**peer), device_id_type=MESH)
    pl.semaphore_wait(barrier, len(peers))

    tasks = {}

    def task(name):
        def keep(step):
            tasks[name] = step
            return step

        return keep

    landed, core_sems = set(), []

    def input_tasks(k):
        b = bufs["x"][k]
        rows = pl.ds(STARTS[k], SPANS[k])

        ax = Straight(m, "x", b.at[core, pl.ds(0, 3), 0, pl.ds(0, 2), :, pl.ds(0, FEAT)])
        az = Straight(m, "z", b.at[core, pl.ds(0, 3), :, pl.ds(0, 2)])
        bz = Straight(m, "z", b.at[core, pl.ds(0, 3), 0, pl.ds(0, 2), :, pl.ds(0, FEAT)])
        bx = Straight(m, "x", b.at[core, pl.ds(0, 3), 0])
        core_sems.append(m.sem())

        eager = k in EAGER_IN
        ax_sems, bz_sems = ({step: m.sem() for step in STEPS} if eager else None for _ in range(2))

        @task(("ax0", k))
        def _():
            ax.send(lambda to: in_ref.at[0:2, rows], lambda step: b.at[core, z, half, 0:2, :, cols(x)], ax_sems)
            if eager:
                az.send(lambda to: in_ref.at[0:2, rows], lambda step: b.at[core, z, half, 0:2, :, cols(x)])

        @task(("bz0", k))
        def _():
            bz.send(lambda to: in_ref.at[2:4, rows], lambda step: b.at[core, z, half, 2:4, :, cols(x)], bz_sems)
            if eager:
                bx.send(lambda to: in_ref.at[2:4, rows], lambda step: b.at[core, z, half, 2:4, :, cols(x)])

        def pass_on(step):
            @task(("ax2" + STEPS[step], k))
            def _():
                q = dev.along("x", RING - step)
                view = b.at[core, z, q // 2, 0:2, :, cols(q)]
                m.wait(view, ax_sems[step])
                az.send(lambda to: view, lambda _: view)

            @task(("bz2" + STEPS[step], k))
            def _():
                view = b.at[core, dev.along("z", RING - step), half, 2:4, :, cols(x)]
                m.wait(view, bz_sems[step])
                bx.send(lambda to: view, lambda _: view)

        if eager:
            for step in STEPS:
                pass_on(step)

        def own_landed():
            if k not in landed:
                m.wait(own_blocks[k], own_sems[k])
                landed.add(k)

        @task(("ax2", k))
        def _():
            own_landed()
            ax.arrive()
            view = b.at[core, z, :, 0:2]
            az.send(lambda to: view, lambda step: view)

        @task(("bz2", k))
        def _():
            own_landed()
            bz.arrive()
            view = b.at[core, :, half, 2:4, :, cols(x)]
            bx.send(lambda to: view, lambda step: view)

        def give(ring, first_row):
            own_landed()
            ring.arrive()
            view = b.at[core, :, :, pl.ds(first_row, 2)]
            m.start(view, view, core_sems[k], core=1 - core)

        tasks["az2", k] = lambda: give(az, 0)
        tasks["bx2", k] = lambda: give(bx, 2)

    for k in CHUNKS:
        input_tasks(k)

    def rows_of(part):
        first, end = part
        return pl.ds(STARTS[first], sum(SPANS[first:end]))

    def cot_tasks(i):
        rows, y_sem, plane_sem = rows_of(COT_PARTS[i]), m.sem(), m.sem()

        @task(("c0", i))
        def _():
            m.here(cot_ref.at[y, rows], cot1.at[y, rows], y_sem)
            for s in (1, 2, 3):
                to = dev.along("y", s)
                m.start(cot_ref.at[to, rows], cot1.at[y, rows], y_sem, y=to)

        @task(("c1", i))
        def _():
            m.wait(cot1.at[:, rows], y_sem)

            def source(to):
                return cot1.at[to["z"], rows, pl.ds(pl.multiple_of((to["x"] // 2) * HID, HID), HID)]

            dst = cot.at[z, half, rows]
            m.here(source(at), dst, plane_sem)
            for to in others:
                m.start(source(to), dst, plane_sem, **to)

        def landed():
            m.wait(cot.at[:, :, rows], plane_sem)

        return landed

    others = [in_plane(*step) for step in plane]
    cot_landed = [cot_tasks(i) for i in range(len(COT_PARTS))]

    def act_tasks(i):
        rows, plane_sem, y_sem = rows_of(ACT_PARTS[i]), m.sem(), m.sem()

        @task(("p0", i))
        def _():
            dst = act1.at[z, rows, pl.ds(pl.multiple_of(half * HID, HID), HID)]
            m.here(act.at[z, half, rows], dst, plane_sem)
            for to in others:
                m.start(act.at[to["z"], to["x"] // 2, rows], dst, plane_sem, **to)

        @task(("p1", i))
        def _():
            m.wait(act1.at[:, rows], plane_sem)
            m.here(act1.at[y, rows], act_ref.at[y, rows], y_sem)
            for s in (1, 2, 3):
                to = dev.along("y", s)
                m.start(act1.at[to, rows], act_ref.at[y, rows], y_sem, y=to)

        tasks["p2", i] = lambda: m.wait(act_ref.at[:, rows], y_sem)

    for i in range(len(ACT_PARTS)):
        act_tasks(i)

    def main_tasks(k):
        b, p, s, d, near = (bufs[name][k] for name in ("x", "p", "s", "d", "ynear"))
        r, rows = SPANS[k], pl.ds(STARTS[k], SPANS[k])
        total = Reduce(m, "y", lambda q, part: p.at[pl.ds(2 * part, 2), :, q], bufs["yfar"][k], near)
        spread = Gather(m, "y", lambda q, part: s.at[pl.ds(2 * part, 2), :, q], s.at[:, :, 0:2])
        cross_sem = m.sem()

        @task(("P", k))
        def _():
            m.wait(b.at[1 - core], core_sems[k])
            if "w" not in landed:
                m.wait(w, w_sem)
                landed.add("w")

            value = jnp.dot(b[0].reshape(32 * r, HID), w[0], preferred_element_type=F32)
            value += jnp.dot(b[1].reshape(32 * r, HID), w[1], preferred_element_type=F32)
            p[...] = value.astype(BF16).reshape(4, 2, 4, r, HID)
            total.begin()

        tasks["R1a", k], tasks["R1b", k] = total.middle_up, total.middle_down

        @task(("G", k))
        def _():
            total.arrive()
            for i, (first, end) in enumerate(COT_PARTS):
                if first <= k < end and ("cot", i) not in landed:
                    cot_landed[i]()
                    landed.add(("cot", i))

            def step(i, carry):
                zz, hh = i // 2, i % 2
                value = p[zz, hh, y].astype(F32)
                value = value + near[0, zz // 2, zz % 2, hh].astype(F32) + near[1, zz // 2, zz % 2, hh].astype(F32)
                a, slope = gelu_and_slope(value, cot[zz, hh, rows].astype(F32))
                act[zz, hh, rows] = a.astype(BF16)
                s[zz, hh, y] = slope.astype(BF16)
                return carry

            lax.fori_loop(0, 8, step, 0)
            spread.begin()

        tasks["A1a", k], tasks["A1b", k] = spread.forward_up, spread.forward_down

        def input_terms(c):
            value = lax.dot_general(
                s[...].reshape(32 * r, HID), w[c], (((1,), (1,)), ((), ())), preferred_element_type=F32
            )
            d[c] = value.astype(BF16).reshape(4, 2, 4, r, HID)

        @task(("Dh", k))
        def _():
            spread.end()
            input_terms(1 - core)
            m.start(d.at[1 - core], bufs["core"][k], cross_sem, core=1 - core)

        @task(("Dl", k))
        def _():
            input_terms(core)

        @task(("W", k))
        def _():
            def tile(c, carry):
                value = lax.dot_general(
                    b[c].reshape(32 * r, HID), s[...].reshape(32 * r, HID),
                    (((0,), (0,)), ((), ())), preferred_element_type=F32,
                )
                if k > 0:
                    value = value + acc[c]
                if k < last:
                    acc[c] = value
                else:
                    dw_ref[c] = value.astype(BF16)
                return carry

            lax.fori_loop(0, 2, tile, 0)

        ax, az, bz, bx = (Straight(m, axis, bufs[name][k]) for name, axis in (("ax", "x"), ("az", "z"), ("bz", "z"), ("bx", "x")))
        land = {name: bufs[name][k] for name in ("ax", "az", "bz", "bx")}

        def pieces(name):
            return {
                "ax": lambda q: d.at[core, :, q // 2, 0:2, :, cols(q)],
                "bz": lambda q: d.at[core, q, :, 2:4],
                "az": lambda q: d.at[core, q, half, 0:2, :, cols(x)],
                "bx": lambda q: d.at[core, z, q // 2, 2:4, :, cols(q)],
            }[name]

        def send(ring, name):
            ring.send(pieces(name), lambda step: land[name].at[step - 1])

        def finish(ring, name):
            ring.arrive()
            add_rows(pieces(name)(at[ring.axis]), *(land[name].at[i] for i in range(3)))

        def x_piece(zz, xx):
            return d.at[core, zz, xx // 2, 0:2, :, cols(xx)]

        def z_piece(zz, xx):
            return d.at[core, zz, xx // 2, 2:4, :, cols(xx)]

        def z_land(i, xx):
            return land["bz"].at[i, xx // 2, :, :, cols(xx)]

        if k in EAGER_OUT:
            x_sems, z_sems = ([m.sem() for _ in range(RING)] for _ in range(2))

        def sum_x(zz, step, *more):
            m.wait(land["ax"].at[:, zz], x_sems[step])
            add_rows(x_piece(zz, x), *(land["ax"].at[i, zz] for i in range(3)), *more)

        def sum_z(xx, step, *more):
            m.wait(z_land(pl.ds(0, 3), xx), z_sems[step])
            add_rows(z_piece(z, xx), *(z_land(i, xx) for i in range(3)), *more)

        def pass_on(step):
            @task(("rx2" + STEPS[step], k))
            def _():
                zz = dev.along("z", step)
                sum_x(zz, step)
                m.start(x_piece(zz, x), land["az"].at[step - 1], az.sem, z=zz)

            @task(("rz2" + STEPS[step], k))
            def _():
                xx = dev.along("x", step)
                sum_z(xx, step)
                m.start(z_piece(z, xx), land["bx"].at[step - 1], bx.sem, x=xx)

        if k in EAGER_OUT:
            for step in STEPS:
                pass_on(step)

        @task(("dx0", k))
        def _():
            m.wait(bufs["core"][k], cross_sem)
            add_rows(d.at[core], bufs["core"][k])
            if k in EAGER_OUT:
                for step in (2, 1, 3, 0):
                    zz, xx = dev.along("z", step), dev.along("x", step)
                    for to in STEPS:
                        q = dev.along("x", to)
                        m.start(x_piece(zz, q), land["ax"].at[to - 1, zz], x_sems[step], x=q)
                    for to in STEPS:
                        q = dev.along("z", to)
                        m.start(z_piece(q, xx), z_land(to - 1, xx), z_sems[step], z=q)
                return
            send(ax, "ax")
            send(bz, "bz")

        @task(("rx2", k))
        def _():
            finish(ax, "ax")
            send(az, "az")

        @task(("rz2", k))
        def _():
            finish(bz, "bz")
            send(bx, "bx")

        @task(("sz2", k))
        def _():
            if k in EAGER_OUT:
                az.arrive()
                sum_x(z, 0, *(land["az"].at[i] for i in range(3)))
            else:
                finish(az, "az")
            dx_ref[0:2, rows, :] = d[core, z, half, 0:2, :, cols(x)]

        @task(("sx2", k))
        def _():
            if k in EAGER_OUT:
                bx.arrive()
                sum_z(x, 0, *(land["bx"].at[i] for i in range(3)))
            else:
                finish(bx, "bx")
            dx_ref[2:4, rows, :] = d[core, z, half, 2:4, :, cols(x)]

    last = len(SPANS) - 1
    for k in CHUNKS:
        main_tasks(k)
    for step in ORDER:
        tasks[step]()
    m.drain()


def on_device(inputs, weight, cotangent):
    shapes = [pltpu.VMEM(shape, BF16) for name, each in scratch_of().items() for shape in each]
    act, dx, dw = pl.pallas_call(
        kernel,
        out_shape=(
            pltpu.VMEM((4, OWN, 2 * HID), BF16),
            pltpu.VMEM((4, OWN, FEAT), BF16),
            pltpu.VMEM((2, HID, HID), BF16),
        ),
        in_specs=[
            pl.BlockSpec(memory_space=pltpu.VMEM),
            pl.BlockSpec(memory_space=pl.ANY),
            pl.BlockSpec(memory_space=pl.ANY),
        ],
        out_specs=(
            pl.BlockSpec(memory_space=pltpu.VMEM),
            pl.BlockSpec(memory_space=pltpu.VMEM),
            pl.BlockSpec(memory_space=pltpu.VMEM),
        ),
        scratch_shapes=[
            *shapes,
            pltpu.VMEM((2, HID, HID), BF16),
            pltpu.VMEM((2, HID, HID), F32),
            pltpu.VMEM((4, OWN, 2 * HID), BF16),
            pltpu.VMEM((4, 2, OWN, HID), BF16),
            pltpu.VMEM((4, 2, OWN, HID), BF16),
            pltpu.VMEM((4, OWN, 2 * HID), BF16),
            pltpu.SemaphoreType.DMA,
            pltpu.SemaphoreType.DMA((N_SEM,)),
        ],
        compiler_params=pltpu.CompilerParams(
            collective_id=0, has_side_effects=True, vmem_limit_bytes=58 * 2**20
        ),
        cost_estimate=pl.CostEstimate(flops=6 * 384 * 1536 * 6144, bytes_accessed=8 * 2**20, transcendentals=0),
    )(
        inputs.reshape(4, OWN, FEAT),
        weight.reshape(2, 2, FEAT, HID),
        cotangent.reshape(4, OWN, 2 * HID),
    )

    def write_out(act_ref, dx_ref, dw_ref, act_out, dx_out, dw_out, sems):
        pairs = [(act_ref, act_out), (dx_ref, dx_out)]
        pairs += [(dw_ref.at[c, pl.ds(lo * FEAT, FEAT)], dw_out.at[lo, c]) for c in range(2) for lo in range(2)]
        copies = [pltpu.make_async_copy(src, dst, sems.at[i]) for i, (src, dst) in enumerate(pairs)]
        for copy in copies:
            copy.start()
        for copy in copies:
            copy.wait()

    act, dx, dw = pl.pallas_call(
        write_out,
        out_shape=(
            jax.ShapeDtypeStruct((4, OWN, 2 * HID), BF16),
            jax.ShapeDtypeStruct((4, OWN, FEAT), BF16),
            jax.ShapeDtypeStruct((2, 2, FEAT, HID), BF16),
        ),
        in_specs=[pl.BlockSpec(memory_space=pl.ANY)] * 3,
        out_specs=(pl.BlockSpec(memory_space=pl.ANY),) * 3,
        scratch_shapes=[pltpu.SemaphoreType.DMA((6,))],
        compiler_params=pltpu.CompilerParams(vmem_limit_bytes=2**20),
    )(act, dx, dw)
    return act.reshape(4 * OWN, 2 * HID), dx.reshape(4 * OWN, FEAT), dw.reshape(4 * FEAT, HID)


def solution(mesh):
    return jax.shard_map(
        on_device,
        mesh=mesh,
        in_specs=(P("gy", ("gz", "gx")), P("gz", ("gx", "gy")), P("gy", ("gx", "gz"))),
        out_specs=(P("gy", ("gx", "gz")), P("gy", ("gz", "gx")), P("gz", ("gx", "gy"))),
        check_vma=False,
    )
```

```python
import functools

import jax
import jax.numpy as jnp
from jax import lax
from jax.experimental import pallas as pl
from jax.experimental.pallas import tpu as pltpu
from jax.sharding import PartitionSpec as P

MESH = pl.DeviceIdType.MESH
F32, BF16 = jnp.float32, jnp.bfloat16
RING = 4
STEPS = {2: "a", 1: "u", 3: "d"}
SPANS = (16, 16, 16, 16, 16, 16)
OWN = sum(SPANS)
STARTS = tuple(sum(SPANS[:k]) for k in range(len(SPANS)))
CHUNKS = range(len(SPANS))
HID = 768
FEAT = 384
COT_PARTS = ((0, 1), (1, 6))
ACT_PARTS = ((0, 3), (3, 5), (5, 6))
EAGER_IN = (0,)
EAGER_OUT = (5,)
N_SEM = 17 * len(SPANS) + 2 * (len(COT_PARTS) + len(ACT_PARTS)) + 2 + 6 * len(EAGER_IN) + 8 * len(EAGER_OUT)
ORDER = (
    ("ax0", 0), ("bz0", 0), ("c0", 0), ("bz0", 2), ("ax0", 2), ("ax2u", 0), ("c0", 1), ("bz2d", 0),
    ("ax2a", 0), ("bz2u", 0), ("bz2a", 0), ("ax2d", 0), ("bz0", 4), ("bz2", 2), ("bz0", 3), ("ax0", 4),
    ("bz0", 1), ("ax2", 2), ("ax0", 1), ("az2", 0), ("ax0", 3), ("ax0", 5), ("bx2", 0), ("P", 0), ("c1", 0),
    ("bz0", 5), ("bx2", 2), ("bz2", 3), ("az2", 2), ("ax2", 3), ("bz2", 1), ("ax2", 1), ("bz2", 4),
    ("R1a", 0), ("R1b", 0), ("P", 2), ("G", 0), ("ax2", 4), ("bx2", 3), ("R1a", 2), ("az2", 3), ("R1b", 2),
    ("P", 3), ("c1", 1), ("bx2", 1), ("az2", 1), ("ax2", 5), ("A1a", 0), ("bx2", 4), ("A1b", 0), ("az2", 4),
    ("P", 1), ("P", 4), ("Dh", 0), ("R1a", 1), ("R1b", 1), ("bz2", 5), ("G", 2), ("G", 1), ("A1b", 2),
    ("az2", 5), ("R1b", 3), ("Dl", 0), ("R1a", 3), ("dx0", 0), ("p0", 0), ("A1a", 2), ("A1a", 1), ("W", 0),
    ("bx2", 5), ("R1a", 4), ("A1b", 1), ("R1b", 4), ("P", 5), ("Dh", 2), ("Dh", 1), ("rz2", 0), ("G", 4),
    ("Dl", 1), ("dx0", 1), ("R1b", 5), ("G", 3), ("A1b", 4), ("p0", 1), ("Dl", 2), ("R1a", 5), ("W", 1),
    ("dx0", 2), ("rx2", 0), ("A1a", 4), ("A1b", 3), ("A1a", 3), ("W", 2), ("G", 5), ("rz2", 1), ("sx2", 0),
    ("p0", 2), ("Dh", 4), ("rz2", 2), ("rx2", 1), ("rx2", 2), ("Dl", 4), ("dx0", 4), ("A1a", 5), ("A1b", 5),
    ("p1", 1), ("Dh", 3), ("sx2", 2), ("sz2", 1), ("Dl", 3), ("dx0", 3), ("Dh", 5), ("p1", 2), ("sz2", 2),
    ("p1", 0), ("Dl", 5), ("dx0", 5), ("W", 3), ("W", 4), ("rx2", 3), ("rz2", 4), ("rx2", 4), ("p2", 2),
    ("rz2", 3), ("rx2a", 5), ("rz2a", 5), ("rz2u", 5), ("sx2", 1), ("rx2u", 5), ("rx2d", 5), ("p2", 1),
    ("sz2", 0), ("rz2d", 5), ("W", 5), ("sx2", 4), ("p2", 0), ("sz2", 3), ("sx2", 3), ("sz2", 4), ("sz2", 5),
    ("sx2", 5),
)


class Device:
    def __init__(self):
        gx, gy, gz = (lax.axis_index(name) for name in ("gx", "gy", "gz"))
        self.core = gx % 2
        self.at = {"x": (gy % 2) * 2 + gx // 2, "y": gz, "z": gy // 2}

    def name(self, core=None, **at):
        at = {**self.at, **at}
        core = self.core if core is None else core
        return {"gx": (at["x"] % 2) * 2 + core, "gy": at["z"] * 2 + at["x"] // 2, "gz": at["y"]}

    def along(self, axis, step):
        return (self.at[axis] + step) % RING


def cols(x):
    return pl.ds(pl.multiple_of((x % 2) * FEAT, FEAT), FEAT)


def gelu_and_slope(value, cotangent):
    scale, cubic = 0.7978845608028654, 0.044715
    square = value * value
    t = jnp.tanh(scale * value * (1.0 + cubic * square))
    half = 0.5 * (1.0 + t)
    slope = half + 0.5 * value * ((1.0 + t) * (1.0 - t)) * (scale + (3.0 * cubic * scale) * square)
    return value * half, cotangent * slope


def add_into(dst, *srcs):
    total = dst[...].astype(F32)
    for src in srcs:
        total = total + src[...].astype(F32)
    dst[...] = total.astype(BF16)


def add_rows(dst, *srcs):
    def step(i, carry):
        add_into(dst.at[i], *(src.at[i] for src in srcs))
        return carry

    lax.fori_loop(0, dst.shape[0], step, 0)


class Moves:
    def __init__(self, device, send, recv):
        self.device, self.send, self.recv = device, send, recv
        self.count = 0
        self.sent = []

    def sem(self):
        self.count += 1
        return self.recv.at[self.count - 1]

    def start(self, src, dst, sem, **to):
        copy = pltpu.make_async_remote_copy(
            src_ref=src, dst_ref=dst, send_sem=self.send, recv_sem=sem,
            device_id=self.device.name(**to), device_id_type=MESH,
        )
        copy.start()
        self.sent.append(copy)

    def here(self, src, dst, sem):
        pltpu.make_async_copy(src, dst, sem).start()

    def wait(self, size, sem):
        pltpu.make_async_copy(size, size, sem).wait()

    def drain(self):
        for copy in self.sent:
            copy.wait_send()
        self.sent = []


class Straight:
    def __init__(self, moves, axis, size):
        self.m, self.axis, self.size, self.sem = moves, axis, size, moves.sem()

    def send(self, src, dst, sems=None):
        for step in STEPS:
            to = self.m.device.along(self.axis, step)
            self.m.start(src(to), dst(step), sems[step] if sems else self.sem, **{self.axis: to})

    def arrive(self):
        self.m.wait(self.size, self.sem)


class Gather:
    def __init__(self, moves, axis, slot, rest):
        self.m, self.axis, self.slot, self.rest = moves, axis, slot, rest
        self.up_sem, self.down_sem, self.rest_sem = moves.sem(), moves.sem(), moves.sem()

    def begin(self):
        d, a = self.m.device, self.axis
        me, up, down = d.at[a], {a: d.along(a, 1)}, {a: d.along(a, 3)}
        first, second = self.slot(me, 0), self.slot(me, 1)
        self.m.start(first, first, self.up_sem, **up)
        self.m.start(second, second, self.down_sem, **down)
        self.m.start(second, second, self.rest_sem, **up)
        self.m.start(first, first, self.rest_sem, **down)

    def forward_up(self):
        d, a = self.m.device, self.axis
        view = self.slot(d.along(a, 3), 0)
        self.m.wait(view, self.up_sem)
        self.m.start(view, view, self.rest_sem, **{a: d.along(a, 1)})

    def forward_down(self):
        d, a = self.m.device, self.axis
        view = self.slot(d.along(a, 1), 1)
        self.m.wait(view, self.down_sem)
        self.m.start(view, view, self.rest_sem, **{a: d.along(a, 3)})

    def end(self):
        self.m.wait(self.rest, self.rest_sem)


class Reduce:
    def __init__(self, moves, axis, piece, far, near):
        self.m, self.axis, self.piece, self.far, self.near = moves, axis, piece, far, near
        self.up_sem, self.down_sem, self.near_sem = moves.sem(), moves.sem(), moves.sem()

    def begin(self):
        d, a, p = self.m.device, self.axis, self.piece
        up, down, across = d.along(a, 1), d.along(a, 3), d.along(a, 2)
        self.m.start(p(across, 0), self.far.at[0], self.up_sem, **{a: up})
        self.m.start(p(across, 1), self.far.at[1], self.down_sem, **{a: down})
        self.m.start(p(up, 1), self.near.at[0, 1], self.near_sem, **{a: up})
        self.m.start(p(down, 0), self.near.at[1, 0], self.near_sem, **{a: down})

    def middle_up(self):
        d, a = self.m.device, self.axis
        up = d.along(a, 1)
        self.m.wait(self.far.at[0], self.up_sem)
        add_rows(self.piece(up, 0), self.far.at[0])
        self.m.start(self.piece(up, 0), self.near.at[0, 0], self.near_sem, **{a: up})

    def middle_down(self):
        d, a = self.m.device, self.axis
        down = d.along(a, 3)
        self.m.wait(self.far.at[1], self.down_sem)
        add_rows(self.piece(down, 1), self.far.at[1])
        self.m.start(self.piece(down, 1), self.near.at[1, 1], self.near_sem, **{a: down})

    def arrive(self):
        self.m.wait(self.near, self.near_sem)


def scratch_of():
    shapes = {}
    for k in CHUNKS:
        r = SPANS[k]
        block = (4, 2, 4, r, HID)
        for name, shape in dict(
            x=(2, *block), p=block, s=block, d=(2, *block), core=block,
            yfar=(2, 2, 2, r, HID), ynear=(2, 2, 2, 2, r, HID),
            ax=(3, 4, 2, r, FEAT), az=(3, 2, r, FEAT), bz=(3, 2, 2, r, HID), bx=(3, 2, r, FEAT),
        ).items():
            shapes.setdefault(name, []).append(shape)
    return shapes


NAMES = tuple(scratch_of())


def kernel(in_ref, w_ref, cot_ref, act_ref, dx_ref, dw_ref, *scratch):
    bufs, rest = {}, list(scratch)
    for name in NAMES:
        bufs[name] = [rest.pop(0) for _ in CHUNKS]
    w, acc, cot1, cot, act, act1, send, recv = rest
    dev = Device()
    core, at = dev.core, dev.at
    x, y, z = at["x"], at["y"], at["z"]
    half = x // 2
    m = Moves(dev, send, recv)
    plane = [(dz, dh) for dz in range(4) for dh in range(2) if (dz, dh) != (0, 0)]

    def in_plane(dz, dh):
        return dict(z=(z + dz) % RING, x=((half + dh) % 2) * 2 + x % 2)

    w_sem, own_sems = m.sem(), [m.sem() for _ in CHUNKS]
    for c in range(2):
        for lo in range(2):
            m.here(w_ref.at[lo, c], w.at[c, pl.ds(lo * FEAT, FEAT)], w_sem)
    own_blocks = [bufs["x"][k].at[core, z, half, :, :, cols(x)] for k in CHUNKS]
    for k in CHUNKS:
        m.here(in_ref.at[:, pl.ds(STARTS[k], SPANS[k])], own_blocks[k], own_sems[k])

    barrier = pltpu.get_barrier_semaphore()
    peers = [dict(core=1 - core), dict(x=dev.along("x", 1)), dict(x=dev.along("x", 3))]
    peers += [dict(y=dev.along("y", s)) for s in (1, 2, 3)] + [in_plane(*step) for step in plane if 0 in step]
    for peer in peers:
        pl.semaphore_signal(barrier, inc=1, device_id=dev.name(**peer), device_id_type=MESH)
    pl.semaphore_wait(barrier, len(peers))

    tasks = {}

    def task(name):
        def keep(step):
            tasks[name] = step
            return step

        return keep

    landed, core_sems = set(), []

    def input_tasks(k):
        b = bufs["x"][k]
        rows = pl.ds(STARTS[k], SPANS[k])

        ax = Straight(m, "x", b.at[core, pl.ds(0, 3), 0, pl.ds(0, 2), :, pl.ds(0, FEAT)])
        az = Straight(m, "z", b.at[core, pl.ds(0, 3), :, pl.ds(0, 2)])
        bz = Straight(m, "z", b.at[core, pl.ds(0, 3), 0, pl.ds(0, 2), :, pl.ds(0, FEAT)])
        bx = Straight(m, "x", b.at[core, pl.ds(0, 3), 0])
        core_sems.append(m.sem())

        eager = k in EAGER_IN
        ax_sems, bz_sems = ({step: m.sem() for step in STEPS} if eager else None for _ in range(2))

        @task(("ax0", k))
        def _():
            ax.send(lambda to: in_ref.at[0:2, rows], lambda step: b.at[core, z, half, 0:2, :, cols(x)], ax_sems)
            if eager:
                az.send(lambda to: in_ref.at[0:2, rows], lambda step: b.at[core, z, half, 0:2, :, cols(x)])

        @task(("bz0", k))
        def _():
            bz.send(lambda to: in_ref.at[2:4, rows], lambda step: b.at[core, z, half, 2:4, :, cols(x)], bz_sems)
            if eager:
                bx.send(lambda to: in_ref.at[2:4, rows], lambda step: b.at[core, z, half, 2:4, :, cols(x)])

        def pass_on(step):
            @task(("ax2" + STEPS[step], k))
            def _():
                q = dev.along("x", RING - step)
                view = b.at[core, z, q // 2, 0:2, :, cols(q)]
                m.wait(view, ax_sems[step])
                az.send(lambda to: view, lambda _: view)

            @task(("bz2" + STEPS[step], k))
            def _():
                view = b.at[core, dev.along("z", RING - step), half, 2:4, :, cols(x)]
                m.wait(view, bz_sems[step])
                bx.send(lambda to: view, lambda _: view)

        if eager:
            for step in STEPS:
                pass_on(step)

        def own_landed():
            if k not in landed:
                m.wait(own_blocks[k], own_sems[k])
                landed.add(k)

        @task(("ax2", k))
        def _():
            own_landed()
            ax.arrive()
            view = b.at[core, z, :, 0:2]
            az.send(lambda to: view, lambda step: view)

        @task(("bz2", k))
        def _():
            own_landed()
            bz.arrive()
            view = b.at[core, :, half, 2:4, :, cols(x)]
            bx.send(lambda to: view, lambda step: view)

        def give(ring, first_row):
            own_landed()
            ring.arrive()
            view = b.at[core, :, :, pl.ds(first_row, 2)]
            m.start(view, view, core_sems[k], core=1 - core)

        tasks["az2", k] = lambda: give(az, 0)
        tasks["bx2", k] = lambda: give(bx, 2)

    for k in CHUNKS:
        input_tasks(k)

    def rows_of(part):
        first, end = part
        return pl.ds(STARTS[first], sum(SPANS[first:end]))

    def cot_tasks(i):
        rows, y_sem, plane_sem = rows_of(COT_PARTS[i]), m.sem(), m.sem()

        @task(("c0", i))
        def _():
            m.here(cot_ref.at[y, rows], cot1.at[y, rows], y_sem)
            for s in (1, 2, 3):
                to = dev.along("y", s)
                m.start(cot_ref.at[to, rows], cot1.at[y, rows], y_sem, y=to)

        @task(("c1", i))
        def _():
            m.wait(cot1.at[:, rows], y_sem)

            def source(to):
                return cot1.at[to["z"], rows, pl.ds(pl.multiple_of((to["x"] // 2) * HID, HID), HID)]

            dst = cot.at[z, half, rows]
            m.here(source(at), dst, plane_sem)
            for to in others:
                m.start(source(to), dst, plane_sem, **to)

        def landed():
            m.wait(cot.at[:, :, rows], plane_sem)

        return landed

    others = [in_plane(*step) for step in plane]
    cot_landed = [cot_tasks(i) for i in range(len(COT_PARTS))]

    def act_tasks(i):
        rows, plane_sem, y_sem = rows_of(ACT_PARTS[i]), m.sem(), m.sem()

        @task(("p0", i))
        def _():
            dst = act1.at[z, rows, pl.ds(pl.multiple_of(half * HID, HID), HID)]
            m.here(act.at[z, half, rows], dst, plane_sem)
            for to in others:
                m.start(act.at[to["z"], to["x"] // 2, rows], dst, plane_sem, **to)

        @task(("p1", i))
        def _():
            m.wait(act1.at[:, rows], plane_sem)
            m.here(act1.at[y, rows], act_ref.at[y, rows], y_sem)
            for s in (1, 2, 3):
                to = dev.along("y", s)
                m.start(act1.at[to, rows], act_ref.at[y, rows], y_sem, y=to)

        tasks["p2", i] = lambda: m.wait(act_ref.at[:, rows], y_sem)

    for i in range(len(ACT_PARTS)):
        act_tasks(i)

    def main_tasks(k):
        b, p, s, d, near = (bufs[name][k] for name in ("x", "p", "s", "d", "ynear"))
        r, rows = SPANS[k], pl.ds(STARTS[k], SPANS[k])
        total = Reduce(m, "y", lambda q, part: p.at[pl.ds(2 * part, 2), :, q], bufs["yfar"][k], near)
        spread = Gather(m, "y", lambda q, part: s.at[pl.ds(2 * part, 2), :, q], s.at[:, :, 0:2])
        cross_sem = m.sem()

        @task(("P", k))
        def _():
            m.wait(b.at[1 - core], core_sems[k])
            if "w" not in landed:
                m.wait(w, w_sem)
                landed.add("w")

            value = jnp.dot(b[0].reshape(32 * r, HID), w[0], preferred_element_type=F32)
            value += jnp.dot(b[1].reshape(32 * r, HID), w[1], preferred_element_type=F32)
            p[...] = value.astype(BF16).reshape(4, 2, 4, r, HID)
            total.begin()

        tasks["R1a", k], tasks["R1b", k] = total.middle_up, total.middle_down

        @task(("G", k))
        def _():
            total.arrive()
            for i, (first, end) in enumerate(COT_PARTS):
                if first <= k < end and ("cot", i) not in landed:
                    cot_landed[i]()
                    landed.add(("cot", i))

            def step(i, carry):
                zz, hh = i // 2, i % 2
                value = p[zz, hh, y].astype(F32)
                value = value + near[0, zz // 2, zz % 2, hh].astype(F32) + near[1, zz // 2, zz % 2, hh].astype(F32)
                a, slope = gelu_and_slope(value, cot[zz, hh, rows].astype(F32))
                act[zz, hh, rows] = a.astype(BF16)
                s[zz, hh, y] = slope.astype(BF16)
                return carry

            lax.fori_loop(0, 8, step, 0)
            spread.begin()

        tasks["A1a", k], tasks["A1b", k] = spread.forward_up, spread.forward_down

        def input_terms(c):
            value = lax.dot_general(
                s[...].reshape(32 * r, HID), w[c], (((1,), (1,)), ((), ())), preferred_element_type=F32
            )
            d[c] = value.astype(BF16).reshape(4, 2, 4, r, HID)

        @task(("Dh", k))
        def _():
            spread.end()
            input_terms(1 - core)
            m.start(d.at[1 - core], bufs["core"][k], cross_sem, core=1 - core)

        @task(("Dl", k))
        def _():
            input_terms(core)

        @task(("W", k))
        def _():
            def tile(c, carry):
                value = lax.dot_general(
                    b[c].reshape(32 * r, HID), s[...].reshape(32 * r, HID),
                    (((0,), (0,)), ((), ())), preferred_element_type=F32,
                )
                if k > 0:
                    value = value + acc[c]
                if k < last:
                    acc[c] = value
                else:
                    dw_ref[c] = value.astype(BF16)
                return carry

            lax.fori_loop(0, 2, tile, 0)

        ax, az, bz, bx = (Straight(m, axis, bufs[name][k]) for name, axis in (("ax", "x"), ("az", "z"), ("bz", "z"), ("bx", "x")))
        land = {name: bufs[name][k] for name in ("ax", "az", "bz", "bx")}

        def pieces(name):
            return {
                "ax": lambda q: d.at[core, :, q // 2, 0:2, :, cols(q)],
                "bz": lambda q: d.at[core, q, :, 2:4],
                "az": lambda q: d.at[core, q, half, 0:2, :, cols(x)],
                "bx": lambda q: d.at[core, z, q // 2, 2:4, :, cols(q)],
            }[name]

        def send(ring, name):
            ring.send(pieces(name), lambda step: land[name].at[step - 1])

        def finish(ring, name):
            ring.arrive()
            add_rows(pieces(name)(at[ring.axis]), *(land[name].at[i] for i in range(3)))

        def x_piece(zz, xx):
            return d.at[core, zz, xx // 2, 0:2, :, cols(xx)]

        def z_piece(zz, xx):
            return d.at[core, zz, xx // 2, 2:4, :, cols(xx)]

        def z_land(i, xx):
            return land["bz"].at[i, xx // 2, :, :, cols(xx)]

        if k in EAGER_OUT:
            x_sems, z_sems = ([m.sem() for _ in range(RING)] for _ in range(2))

        def sum_x(zz, step, *more):
            m.wait(land["ax"].at[:, zz], x_sems[step])
            add_rows(x_piece(zz, x), *(land["ax"].at[i, zz] for i in range(3)), *more)

        def sum_z(xx, step, *more):
            m.wait(z_land(pl.ds(0, 3), xx), z_sems[step])
            add_rows(z_piece(z, xx), *(z_land(i, xx) for i in range(3)), *more)

        def pass_on(step):
            @task(("rx2" + STEPS[step], k))
            def _():
                zz = dev.along("z", step)
                sum_x(zz, step)
                m.start(x_piece(zz, x), land["az"].at[step - 1], az.sem, z=zz)

            @task(("rz2" + STEPS[step], k))
            def _():
                xx = dev.along("x", step)
                sum_z(xx, step)
                m.start(z_piece(z, xx), land["bx"].at[step - 1], bx.sem, x=xx)

        if k in EAGER_OUT:
            for step in STEPS:
                pass_on(step)

        @task(("dx0", k))
        def _():
            m.wait(bufs["core"][k], cross_sem)
            add_rows(d.at[core], bufs["core"][k])
            if k in EAGER_OUT:
                for step in (2, 1, 3, 0):
                    zz, xx = dev.along("z", step), dev.along("x", step)
                    for to in STEPS:
                        q = dev.along("x", to)
                        m.start(x_piece(zz, q), land["ax"].at[to - 1, zz], x_sems[step], x=q)
                    for to in STEPS:
                        q = dev.along("z", to)
                        m.start(z_piece(q, xx), z_land(to - 1, xx), z_sems[step], z=q)
                return
            send(ax, "ax")
            send(bz, "bz")

        @task(("rx2", k))
        def _():
            finish(ax, "ax")
            send(az, "az")

        @task(("rz2", k))
        def _():
            finish(bz, "bz")
            send(bx, "bx")

        @task(("sz2", k))
        def _():
            if k in EAGER_OUT:
                az.arrive()
                sum_x(z, 0, *(land["az"].at[i] for i in range(3)))
            else:
                finish(az, "az")
            dx_ref[0:2, rows, :] = d[core, z, half, 0:2, :, cols(x)]

        @task(("sx2", k))
        def _():
            if k in EAGER_OUT:
                bx.arrive()
                sum_z(x, 0, *(land["bx"].at[i] for i in range(3)))
            else:
                finish(bx, "bx")
            dx_ref[2:4, rows, :] = d[core, z, half, 2:4, :, cols(x)]

    last = len(SPANS) - 1
    for k in CHUNKS:
        main_tasks(k)
    for step in ORDER:
        tasks[step]()
    m.drain()


def on_device(inputs, weight, cotangent):
    shapes = [pltpu.VMEM(shape, BF16) for name, each in scratch_of().items() for shape in each]
    act, dx, dw = pl.pallas_call(
        kernel,
        out_shape=(
            pltpu.VMEM((4, OWN, 2 * HID), BF16),
            pltpu.VMEM((4, OWN, FEAT), BF16),
            pltpu.VMEM((2, HID, HID), BF16),
        ),
        in_specs=[
            pl.BlockSpec(memory_space=pltpu.VMEM),
            pl.BlockSpec(memory_space=pl.ANY),
            pl.BlockSpec(memory_space=pl.ANY),
        ],
        out_specs=(
            pl.BlockSpec(memory_space=pltpu.VMEM),
            pl.BlockSpec(memory_space=pltpu.VMEM),
            pl.BlockSpec(memory_space=pltpu.VMEM),
        ),
        scratch_shapes=[
            *shapes,
            pltpu.VMEM((2, HID, HID), BF16),
            pltpu.VMEM((2, HID, HID), F32),
            pltpu.VMEM((4, OWN, 2 * HID), BF16),
            pltpu.VMEM((4, 2, OWN, HID), BF16),
            pltpu.VMEM((4, 2, OWN, HID), BF16),
            pltpu.VMEM((4, OWN, 2 * HID), BF16),
            pltpu.SemaphoreType.DMA,
            pltpu.SemaphoreType.DMA((N_SEM,)),
        ],
        compiler_params=pltpu.CompilerParams(
            collective_id=0, has_side_effects=True, vmem_limit_bytes=58 * 2**20
        ),
        cost_estimate=pl.CostEstimate(flops=6 * 384 * 1536 * 6144, bytes_accessed=8 * 2**20, transcendentals=0),
    )(
        inputs.reshape(4, OWN, FEAT),
        weight.reshape(2, 2, FEAT, HID),
        cotangent.reshape(4, OWN, 2 * HID),
    )

    def write_out(act_ref, dx_ref, dw_ref, act_out, dx_out, dw_out, sems):
        pairs = [(act_ref, act_out), (dx_ref, dx_out)]
        pairs += [(dw_ref.at[c, pl.ds(lo * FEAT, FEAT)], dw_out.at[lo, c]) for c in range(2) for lo in range(2)]
        copies = [pltpu.make_async_copy(src, dst, sems.at[i]) for i, (src, dst) in enumerate(pairs)]
        for copy in copies:
            copy.start()
        for copy in copies:
            copy.wait()

    act, dx, dw = pl.pallas_call(
        write_out,
        out_shape=(
            jax.ShapeDtypeStruct((4, OWN, 2 * HID), BF16),
            jax.ShapeDtypeStruct((4, OWN, FEAT), BF16),
            jax.ShapeDtypeStruct((2, 2, FEAT, HID), BF16),
        ),
        in_specs=[pl.BlockSpec(memory_space=pl.ANY)] * 3,
        out_specs=(pl.BlockSpec(memory_space=pl.ANY),) * 3,
        scratch_shapes=[pltpu.SemaphoreType.DMA((6,))],
        compiler_params=pltpu.CompilerParams(vmem_limit_bytes=2**20),
    )(act, dx, dw)
    return act.reshape(4 * OWN, 2 * HID), dx.reshape(4 * OWN, FEAT), dw.reshape(4 * FEAT, HID)


def solution(mesh):
    return jax.shard_map(
        on_device,
        mesh=mesh,
        in_specs=(P("gy", ("gz", "gx")), P("gz", ("gx", "gy")), P("gy", ("gx", "gz"))),
        out_specs=(P("gy", ("gx", "gz")), P("gy", ("gz", "gx")), P("gz", ("gx", "gy"))),
        check_vma=False,
    )
```
